256 devices in a mesh: row: 8 (over x, core), col: 32 (over z, y).
Axes of the slice: x: 4, y: 4, z: 8, core: 2. Of those that a mesh axis runs over, the one named last changes fastest.
Arguments:
- matrix: float32 [8, 8, 256, 2, 32, 256], P(None, 'row', None, None, 'col'), as said below
- pattern: int32 [64, 64], replicated, may hold values from 0 to 1, as said below
Outputs:
- factored: float32 [8, 8, 256, 2, 32, 256], P(None, 'row', None, None, 'col')
The draws below stay inside these ranges and needn't reach their ends.
Inputs may be any that keep to these rules, and one draw needn't show every extreme that they name: pattern is symmetric with ones on its diagonal and pattern[1, 0] = 1; writing c0 and c1 for its columns 0 and 1, c1[I] >= c0[I], and pattern[I, J] = 1 wherever c0[I] = c0[J] = 1 or c1[I] = c1[J] = 1 with I, J >= 1 (closed under the fill of the two panels). matrix is symmetric positive definite.
All inputs are finite; a program needn't handle non-finite values.
Results may differ from the reference program's by a relative error of at most 0.0001.
Values sent between devices are 32-bit elements; how exact they have to be, the bound alone decides.
No kernel may reach another device: no remote copies, remote signals or barrier semaphores. Data moves between devices by JAX's collectives and lax.ppermute only.
A program may use at most 64 MiB of HBM per device.

```python
import jax
import jax.numpy as jnp
from jax import lax

BLK = 256
CB = 2
NB = 64
RB = 8
N_ROW = 8
N_COL = 32


def shared_pattern(key):
    base_key = jax.random.fold_in(key, 11)
    base = jax.random.randint(base_key, (NB, NB), 0, 5)
    lowered = jnp.tril((base < 2).astype(jnp.int32), -1)
    symmetric = lowered + lowered.T + jnp.eye(NB, dtype=jnp.int32)
    first = jax.random.randint(jax.random.fold_in(key, 12), (NB,), 0, 2)
    first = first.at[0].set(1).at[1].set(1)
    second = jax.random.randint(jax.random.fold_in(key, 13), (NB,), 0, 2)
    second = jnp.maximum(second, first)
    filled = jnp.maximum(symmetric, first[:, None] * first[None, :])
    filled = jnp.maximum(filled, second[:, None] * second[None, :])
    filled = filled.at[:, 0].set(first).at[0, :].set(first)
    filled = filled.at[:, 1].set(second).at[1, :].set(second)
    return filled.astype(jnp.int32)


def draw_pattern(key, part):
    return shared_pattern(key)


def draw_matrix(key, part):
    blocks = shared_pattern(key)
    key = jax.random.fold_in(key, 5)
    order = NB * BLK
    raw = jax.random.normal(jax.random.fold_in(key, 1), (order, order), jnp.float32)
    coupling = jax.random.normal(jax.random.fold_in(key, 4), (order, 2 * BLK), jnp.float32)
    sym = (raw + raw.T) * 0.70710677
    mask = jnp.repeat(jnp.repeat(blocks, BLK, axis=0), BLK, axis=1).astype(jnp.float32)
    rows_first = jnp.repeat(blocks[:, 0], BLK).astype(jnp.float32)
    rows_second = jnp.repeat(blocks[:, 1], BLK).astype(jnp.float32)
    coupling = jnp.concatenate([coupling[:, :BLK] * rows_first[:, None], coupling[:, BLK:] * rows_second[:, None]], axis=1)
    filling = jnp.dot(coupling, coupling.T, precision=lax.Precision.HIGHEST)
    filling = (filling + filling.T) * 0.5
    rough = jax.random.uniform(jax.random.fold_in(key, 2), (order,), jnp.float32, 2.5, 4.0)
    diag_vals = rough * jnp.sqrt(jnp.float32(order))
    idx = jnp.arange(order)
    full = jnp.where(idx[:, None] == idx[None, :], diag_vals[:, None], sym * mask) + filling
    return full.reshape(RB, N_ROW, BLK, CB, N_COL, BLK).astype(jnp.float32)


def setup_inputs(seed: int = 0) -> dict:
    keys = jax.random.split(jax.random.key(seed), 3)
    return {
        "matrix": draw_matrix(jax.random.fold_in(keys[2], 71), 0),
        "pattern": draw_pattern(jax.random.fold_in(keys[2], 71), 0),
    }


def reference(matrix, pattern):
    blocks = matrix.reshape(NB, BLK, NB, BLK)
    ids = jnp.arange(NB)
    lower_blocks = (ids[:, None] >= ids[None, :]).astype(jnp.float32)
    for k in range(2):
        pivot = jnp.linalg.cholesky(blocks[k, :, k, :])
        column = blocks[:, :, k, :]
        stacked = column.transpose(2, 0, 1).reshape(BLK, NB * BLK)
        solved = lax.linalg.triangular_solve(pivot, stacked, left_side=True, lower=True)
        solved = solved.reshape(BLK, NB, BLK).transpose(1, 2, 0)
        panel = jnp.where((ids > k)[:, None, None], solved, jnp.zeros_like(solved))
        panel = jnp.where((ids == k)[:, None, None], pivot[None, :, :], panel)
        weight = pattern.astype(jnp.float32) * lower_blocks * (ids[None, :] > k).astype(jnp.float32)
        update = jnp.einsum('iab,jcb->iajc', panel, panel, precision=lax.Precision.HIGHEST)
        blocks = blocks - weight[:, None, :, None] * update
        blocks = blocks.at[:, :, k, :].set(panel)
    blocks = blocks * lower_blocks[:, None, :, None]
    return blocks.reshape(RB, N_ROW, BLK, CB, N_COL, BLK)
```

```python
import functools

import jax
import jax.numpy as jnp
import numpy as np
from jax import lax
from jax.experimental import pallas as pl
from jax.experimental.pallas import tpu as pltpu
from jax.sharding import PartitionSpec as P

AXES = ("row", "col")
NX, NCORE, NZ, NY = (4, 2, 8, 4)
BLK = 256
HALF = 128
STEP = 8
DEVICE = np.arange(NX * NCORE * NZ * NY).reshape(NX, NCORE, NZ, NY)
VMEM = pl.BlockSpec(memory_space=pltpu.VMEM)


def dot(a, b, contract=((1,), (0,))):
    return lax.dot_general(a, b, (contract, ((), ())), precision=lax.Precision.HIGHEST, preferred_element_type=jnp.float32)


def invert_factor(block):
    n = block.shape[0]
    lane = lax.broadcasted_iota(jnp.int32, (8, n), 1)
    sub = lax.broadcasted_iota(jnp.int32, (8, n), 0)
    rows = [block[8 * g : 8 * g + 8, :] for g in range(n // 8)]
    for first in range(0, n, STEP):
        top, at = divmod(first, 8)
        inside = (lane >= first) & (lane < first + STEP)
        low = range(top, n // 8)
        column = {
            g: [jnp.broadcast_to(rows[g][:, first + k : first + k + 1], (8, n)) for k in range(STEP)] for g in low
        }
        pivot = [
            [jnp.broadcast_to(column[top][k][at + i : at + i + 1, :], (8, n)) for k in range(i + 1)]
            for i in range(STEP)
        ]
        upper = [
            jnp.where(
                inside,
                (lane == first + k).astype(jnp.float32),
                jnp.broadcast_to(rows[top][at + k : at + k + 1, :], (8, n)),
            )
            for k in range(STEP)
        ]
        inverse = []
        for k in range(STEP):
            inverse.append(1.0 / pivot[k][k])
            for i in range(k + 1, STEP):
                ratio = pivot[i][k] * inverse[k]
                for m in range(k + 1, i + 1):
                    pivot[i][m] = pivot[i][m] - ratio * pivot[m][k]
                upper[i] = upper[i] - ratio * upper[k]
                for g in low:
                    column[g][i] = column[g][i] - ratio * column[g][k]
        scaled = [upper[k] * inverse[k] for k in range(STEP)]
        for g in low:
            left = jnp.where(inside, 0.0, rows[g])
            for k in range(STEP):
                left = left - column[g][k] * scaled[k]
            if g == top:
                done = rows[g]
                for k in range(STEP):
                    done = jnp.where(sub == at + k, upper[k] * lax.rsqrt(pivot[k][k]), done)
                left = jnp.where(sub >= at + STEP, left, done)
            rows[g] = left
    whole = jnp.concatenate(rows, axis=0)
    r = lax.broadcasted_iota(jnp.int32, (n, n), 0)
    c = lax.broadcasted_iota(jnp.int32, (n, n), 1)
    return jnp.where(c <= r, whole, 0.0)


def invert_pair(block, out):
    h = HALF
    top = invert_factor(block[:h, :h])
    link = dot(top, block[:h, h:])
    low = invert_factor(block[h:, h:] - dot(link, link, ((0,), (0,))))
    out[:h, :h] = top
    out[:h, h:] = jnp.zeros((h, h), jnp.float32)
    out[h:, :h] = -dot(dot(low, link, ((1,), (1,))), top)
    out[h:, h:] = low


def pivots_kernel(a00, a01, a11, inv00, u01, inv11):
    invert_pair(a00[...], inv00)
    link = dot(inv00[...], a01[...])
    u01[...] = link
    invert_pair(a11[...] - dot(link, link, ((0,), (0,))), inv11)


def factor_pivots(a00, a01, a11):
    shape = jax.ShapeDtypeStruct((BLK, BLK), jnp.float32)
    return pl.pallas_call(
        pivots_kernel,
        out_shape=(shape, shape, shape),
        in_specs=[VMEM] * 3,
        out_specs=[VMEM] * 3,
        compiler_params=pltpu.CompilerParams(vmem_limit_bytes=32 << 20),
        cost_estimate=pl.CostEstimate(flops=25_000_000_000, bytes_accessed=1 << 20, transcendentals=0),
        name="factor_pivots",
    )(a00, a01, a11)


def update_kernel(ids, pattern, local, g, y, inv00, u01, inv11, out, back0, back1, cols):
    j, h = (pl.program_id(0), pl.program_id(1))
    p, q = (ids[0], ids[1])
    row_id = (j + 4 * h) * 8 + p

    @pl.when((j == 0) & (h == 0))
    def _():
        back0[...] = inv00[...].T
        back1[...] = inv11[...].T
        for c in range(2):
            w = pattern[32 * c + q, 1].astype(jnp.float32)
            first = dot(inv00[...], y[0, c])
            cols[c, :BLK, :] = first
            cols[c, BLK:, :] = dot(inv11[...], y[1, c] - w * dot(u01[...], first, ((0,), (0,))))

    slots = [(ids[2] + 4 - 2 * h - part) % 4 for part in range(2)]
    raw = [jnp.concatenate([g[0, k, slots[0]], g[0, k, slots[1]]], axis=0) for k in range(2)]
    w1 = pattern[row_id, 1].astype(jnp.float32)
    x0 = dot(raw[0], back0[...])
    x1 = dot(raw[1] - w1 * dot(x0, u01[...]), back1[...])
    x = jnp.concatenate([x0, x1], axis=1)
    for c in range(2):
        col_id = 32 * c + q
        places = [pl.ds(2 * c + side, BLK, stride=4) for side in range(2)]

        def put(value):
            for side in range(2):
                out[0, places[side], :] = value[:, side * HALF : (side + 1) * HALF]

        panel = col_id < 2
        lower = row_id >= col_id
        changed = lower & ~panel & (pattern[row_id, col_id] != 0)

        @pl.when(panel)
        def _():
            r = lax.broadcasted_iota(jnp.int32, (BLK, BLK), 0)
            s = lax.broadcasted_iota(jnp.int32, (BLK, BLK), 1)
            kept = (row_id > col_id) | ((row_id == col_id) & (s <= r))
            put(jnp.where(kept, jnp.where(col_id == 0, x0, x1), 0.0))

        @pl.when(~panel & ~lower)
        def _():
            put(jnp.zeros((BLK, BLK), jnp.float32))

        @pl.when(changed)
        def _():
            for side in range(2):
                lanes = slice(side * HALF, (side + 1) * HALF)
                out[0, places[side], :] = local[0, places[side], :] - dot(x, cols[c, :, lanes])

        @pl.when(lower & ~panel & ~changed)
        def _():
            for side in range(2):
                out[0, places[side], :] = local[0, places[side], :]


def update(ids, pattern, local, g, y, inv00, u01, inv11):
    whole = lambda *shape: pl.BlockSpec(shape, lambda j, h, *_: (0,) * len(shape))
    return pl.pallas_call(
        update_kernel,
        out_shape=jax.ShapeDtypeStruct(local.shape, jnp.float32),
        grid_spec=pltpu.PrefetchScalarGridSpec(
            num_scalar_prefetch=2,
            grid=(4, 2),
            in_specs=[
                pl.BlockSpec((1, 4 * BLK, HALF), lambda j, h, *_: (j + 4 * h, 0, 0)),
                pl.BlockSpec((1, 2, 4, HALF, BLK), lambda j, h, *_: (j, 0, 0, 0, 0)),
                whole(2, 2, BLK, BLK),
                whole(BLK, BLK),
                whole(BLK, BLK),
                whole(BLK, BLK),
            ],
            out_specs=pl.BlockSpec((1, 4 * BLK, HALF), lambda j, h, *_: (j + 4 * h, 0, 0)),
            scratch_shapes=[
                pltpu.VMEM((BLK, BLK), jnp.float32),
                pltpu.VMEM((BLK, BLK), jnp.float32),
                pltpu.VMEM((2, 2 * BLK, BLK), jnp.float32),
            ],
        ),
        compiler_params=pltpu.CompilerParams(vmem_limit_bytes=32 << 20),
        cost_estimate=pl.CostEstimate(flops=12_000_000_000, bytes_accessed=14 << 20, transcendentals=0),
        name="update",
    )(ids, pattern, local, g, y, inv00, u01, inv11)


def shifted(value, x=0, core=0, z=0, y=0, where=None):
    pairs = []
    for place in np.ndindex(NX, NCORE, NZ, NY):
        if where is None or where(*place):
            a, b, c, d = place
            to = ((a + x) % NX, (b + core) % NCORE, (c + z) % NZ, (d + y) % NY)
            pairs.append((int(DEVICE[place]), int(DEVICE[to])))
    return lax.ppermute(value, AXES, pairs)


ROUNDS = (
    tuple(dict(z=k) for k in (2, 6, 4)),
    (dict(z=1),),
    tuple(dict(y=k) for k in (1, 3, 2)),
    tuple(dict(x=k) for k in (1, 3, 2)),
    (dict(core=1),),
)


def spread(value, root):
    have = {root}
    names = ("x", "core", "z", "y")
    sizes = (NX, NCORE, NZ, NY)
    for moves in ROUNDS:
        holders = frozenset(have)
        got = [shifted(value, where=lambda *place: place in holders, **move) for move in moves]
        for move in moves:
            have |= {tuple((s + move.get(n, 0)) % m for s, n, m in zip(place, names, sizes)) for place in holders}
        for one in got:
            value = value + one
    return value


def per_device(matrix, pattern):
    p = lax.axis_index("row")
    q = lax.axis_index("col")
    x, core, z, y = (p // NCORE, p % NCORE, q // NY, q % NY)
    local = matrix.reshape(8, 4 * BLK, HALF)
    head = matrix[0, 0, :, :, 0, :].transpose(1, 0, 2)
    turned = head.transpose(0, 2, 1).reshape(4, HALF, BLK)

    parts = []
    for m in range(4):
        pairs = [(32 * c + s, (s % 8) * 32 + 8 * (s // 8) + 4 * c + m) for c in range(2) for s in range(32)]
        parts.append(lax.ppermute(turned[m], AXES, pairs))
    mine = parts[0] + parts[1] + parts[2] + parts[3]
    quarters = jnp.stack([mine] + [shifted(mine, y=k) for k in (1, 2, 3)])
    groups = [[NY * b + a for b in range(NZ)] for a in range(NY)]
    rows = lax.all_gather(quarters, "col", axis=0, axis_index_groups=groups)
    rows = rows.reshape(4, 2, 4, HALF, BLK)

    here = (x == 0) & (z == 0)
    own = head[0]
    a00 = spread(jnp.where(here & (core == 0) & (y == 0), own, 0.0), (0, 0, 0, 0))
    below = shifted(own, core=1, where=lambda *place: place == (0, 1, 0, 1))
    pair = jnp.where(here & (core == 0) & (y == 1), jnp.stack([own, below]), 0.0)
    pair = spread(pair, (0, 0, 0, 1))

    first = jnp.where(x == 0, head, 0.0)
    cols = first
    for k in (1, 3, 2):
        cols = cols + shifted(first, x=k, where=lambda a, *_: a == 0)
    other = shifted(cols, core=1)
    panel = jnp.where(core == 0, jnp.stack([cols, other]), jnp.stack([other, cols]))

    inv00, u01, inv11 = factor_pivots(a00, pair[0], pair[1])
    ids = jnp.stack([p, q, y]).astype(jnp.int32)
    out = update(ids, pattern, local, rows, panel, inv00, u01, inv11)
    return out.reshape(matrix.shape)


def solution(mesh):
    return jax.shard_map(
        per_device,
        mesh=mesh,
        in_specs=(P(None, "row", None, None, "col", None), P()),
        out_specs=P(None, "row", None, None, "col", None),
        check_vma=False,
    )
```

```python
import functools

import jax
import jax.numpy as jnp
import numpy as np
from jax import lax
from jax.experimental import pallas as pl
from jax.experimental.pallas import tpu as pltpu
from jax.sharding import PartitionSpec as P

AXES = ("row", "col")
NX, NCORE, NZ, NY = (4, 2, 8, 4)
BLK = 256
HALF = 128
STEP = 8
DEVICE = np.arange(NX * NCORE * NZ * NY).reshape(NX, NCORE, NZ, NY)
VMEM = pl.BlockSpec(memory_space=pltpu.VMEM)


def dot(a, b, contract=((1,), (0,))):
    return lax.dot_general(a, b, (contract, ((), ())), precision=lax.Precision.HIGHEST, preferred_element_type=jnp.float32)


def invert_factor(block):
    n = block.shape[0]
    lane = lax.broadcasted_iota(jnp.int32, (8, n), 1)
    sub = lax.broadcasted_iota(jnp.int32, (8, n), 0)
    rows = [block[8 * g : 8 * g + 8, :] for g in range(n // 8)]
    for first in range(0, n, STEP):
        top, at = divmod(first, 8)
        inside = (lane >= first) & (lane < first + STEP)
        low = range(top, n // 8)
        column = {
            g: [jnp.broadcast_to(rows[g][:, first + k : first + k + 1], (8, n)) for k in range(STEP)] for g in low
        }
        pivot = [
            [jnp.broadcast_to(column[top][k][at + i : at + i + 1, :], (8, n)) for k in range(i + 1)]
            for i in range(STEP)
        ]
        upper = [
            jnp.where(
                inside,
                (lane == first + k).astype(jnp.float32),
                jnp.broadcast_to(rows[top][at + k : at + k + 1, :], (8, n)),
            )
            for k in range(STEP)
        ]
        inverse = []
        for k in range(STEP):
            inverse.append(1.0 / pivot[k][k])
            for i in range(k + 1, STEP):
                ratio = pivot[i][k] * inverse[k]
                for m in range(k + 1, i + 1):
                    pivot[i][m] = pivot[i][m] - ratio * pivot[m][k]
                upper[i] = upper[i] - ratio * upper[k]
                for g in low:
                    column[g][i] = column[g][i] - ratio * column[g][k]
        scaled = [upper[k] * inverse[k] for k in range(STEP)]
        for g in low:
            left = jnp.where(inside, 0.0, rows[g])
            for k in range(STEP):
                left = left - column[g][k] * scaled[k]
            if g == top:
                done = rows[g]
                for k in range(STEP):
                    done = jnp.where(sub == at + k, upper[k] * lax.rsqrt(pivot[k][k]), done)
                left = jnp.where(sub >= at + STEP, left, done)
            rows[g] = left
    whole = jnp.concatenate(rows, axis=0)
    r = lax.broadcasted_iota(jnp.int32, (n, n), 0)
    c = lax.broadcasted_iota(jnp.int32, (n, n), 1)
    return jnp.where(c <= r, whole, 0.0)


def invert_pair(block, out):
    h = HALF
    top = invert_factor(block[:h, :h])
    link = dot(top, block[:h, h:])
    low = invert_factor(block[h:, h:] - dot(link, link, ((0,), (0,))))
    out[:h, :h] = top
    out[:h, h:] = jnp.zeros((h, h), jnp.float32)
    out[h:, :h] = -dot(dot(low, link, ((1,), (1,))), top)
    out[h:, h:] = low


def first_kernel(a00, inv00):
    invert_pair(a00[...], inv00)


def second_kernel(inv00, a01, a11, u01, inv11):
    link = dot(inv00[...], a01[...])
    u01[...] = link
    invert_pair(a11[...] - dot(link, link, ((0,), (0,))), inv11)


def on_blocks(kernel, outs, name, *blocks):
    shape = jax.ShapeDtypeStruct((BLK, BLK), jnp.float32)
    return pl.pallas_call(
        kernel,
        out_shape=(shape,) * outs,
        in_specs=[VMEM] * len(blocks),
        out_specs=[VMEM] * outs,
        compiler_params=pltpu.CompilerParams(vmem_limit_bytes=32 << 20),
        cost_estimate=pl.CostEstimate(flops=12_000_000_000, bytes_accessed=1 << 20, transcendentals=0),
        name=name,
    )(*blocks)


LEFT = {3: (0, 0, 1, 0, 1, 2), 2: (0, 1, 0)}
RIGHT = {3: (0, 1, 0, 2, 1, 0), 2: (0, 0, 1)}


def split(value, count=3):
    parts = []
    for number in range(count):
        parts.append(value.astype(jnp.bfloat16))
        if number + 1 < count:
            value = value - parts[-1].astype(jnp.float32)
    return parts


def product(left, right, count=3):
    a = jnp.concatenate([left[k] for k in LEFT[count]], axis=1)
    b = jnp.concatenate([right[k] for k in RIGHT[count]], axis=0)
    return jnp.dot(a, b, preferred_element_type=jnp.float32)


def columns_kernel(ids, pattern, y0, y1, inv00, u01, inv11, back0, back1, link, cols):
    for out, value in ((back0, inv00[...].T), (back1, inv11[...].T), (link, u01[...])):
        for number, part in enumerate(split(value)):
            out[number] = part
    q = ids[1]
    swap = ids[2] == 1
    inverse0, inverse1, down = (split(inv00[...]), split(inv11[...]), split(u01[...].T))
    for c in range(2):
        w = pattern[32 * c + q, 1].astype(jnp.float32)
        first = product(inverse0, split(jnp.where(swap, y1[c], y0[c])))
        left = jnp.where(swap, y0[c], y1[c]) - w * product(down, split(first))
        second = product(inverse1, split(left))
        for k, value in enumerate((first, second)):
            for number, part in enumerate(split(value, 2)):
                cols[c, number, k * BLK : (k + 1) * BLK, :] = part


def solve_columns(ids, pattern, y0, y1, inv00, u01, inv11):
    smem = pl.BlockSpec(memory_space=pltpu.SMEM)
    parts = jax.ShapeDtypeStruct((3, BLK, BLK), jnp.bfloat16)
    return pl.pallas_call(
        columns_kernel,
        out_shape=(parts, parts, parts, jax.ShapeDtypeStruct((2, 2, 2 * BLK, BLK), jnp.bfloat16)),
        in_specs=[smem, smem] + [VMEM] * 5,
        out_specs=[VMEM] * 4,
        compiler_params=pltpu.CompilerParams(vmem_limit_bytes=32 << 20),
        cost_estimate=pl.CostEstimate(flops=3_000_000_000, bytes_accessed=4 << 20, transcendentals=0),
        name="solve_columns",
    )(ids, pattern, y0, y1, inv00, u01, inv11)


def update_kernel(ids, pattern, local, g, back0, back1, link, cols, out):
    j = pl.program_id(0)
    p, q = (ids[0], ids[1])
    slots = [(ids[3] + 4 - m) % 4 for m in range(4)]
    raw = [jnp.concatenate([g[k, slot] for slot in slots], axis=0) for k in range(2)]
    first = product(split(raw[0]), back0)
    x0 = split(first)
    linked = product(x0, link)
    w = [pattern[(j + 4 * h) * 8 + p, 1].astype(jnp.float32) for h in range(2)]
    left = [raw[1][h * BLK : (h + 1) * BLK] - w[h] * linked[h * BLK : (h + 1) * BLK] for h in range(2)]
    second = product(split(jnp.concatenate(left, axis=0)), back1)
    x1 = split(second, 2)
    solved = [jnp.concatenate([x0[k], x1[k]], axis=1) for k in range(2)]
    for h in range(2):
        row_id = (j + 4 * h) * 8 + p
        rows = slice(h * BLK, (h + 1) * BLK)
        for c in range(2):
            col_id = 32 * c + q
            places = [pl.ds(2 * c + side, BLK, stride=4) for side in range(2)]
            halves = [slice(side * HALF, (side + 1) * HALF) for side in range(2)]
            panel = col_id < 2
            lower = row_id >= col_id
            changed = lower & ~panel & (pattern[row_id, col_id] != 0)

            @pl.when(panel)
            def _():
                r = lax.broadcasted_iota(jnp.int32, (BLK, BLK), 0)
                s = lax.broadcasted_iota(jnp.int32, (BLK, BLK), 1)
                kept = (row_id > col_id) | ((row_id == col_id) & (s <= r))
                value = jnp.where(kept, jnp.where(col_id == 0, first[rows], second[rows]), 0.0)
                for side in range(2):
                    out[h, 0, places[side], :] = value[:, halves[side]]

            @pl.when(~panel & ~lower)
            def _():
                for side in range(2):
                    out[h, 0, places[side], :] = jnp.zeros((BLK, HALF), jnp.float32)

            @pl.when(changed)
            def _():
                change = product([part[rows] for part in solved], cols[c], 2)
                for side in range(2):
                    out[h, 0, places[side], :] = local[h, 0, places[side], :] - change[:, halves[side]]

            @pl.when(lower & ~panel & ~changed)
            def _():
                for side in range(2):
                    out[h, 0, places[side], :] = local[h, 0, places[side], :]


def update(ids, pattern, local, g, back0, back1, link, cols):
    whole = lambda *shape: pl.BlockSpec(shape, lambda j, *_: (0,) * len(shape))
    block = pl.BlockSpec((2, 1, 4 * BLK, HALF), lambda j, *_: (0, j, 0, 0))
    return pl.pallas_call(
        update_kernel,
        out_shape=jax.ShapeDtypeStruct(local.shape, jnp.float32),
        grid_spec=pltpu.PrefetchScalarGridSpec(
            num_scalar_prefetch=2,
            grid=(4,),
            in_specs=[
                block,
                pl.BlockSpec((2, 4, HALF, BLK), lambda j, *_: (j, 0, 0, 0)),
                *[whole(3, BLK, BLK)] * 3,
                whole(2, 2, 2 * BLK, BLK),
            ],
            out_specs=block,
        ),
        compiler_params=pltpu.CompilerParams(vmem_limit_bytes=40 << 20),
        cost_estimate=pl.CostEstimate(flops=12_000_000_000, bytes_accessed=14 << 20, transcendentals=0),
        name="update",
    )(ids, pattern, local, g, back0, back1, link, cols)


def shifted(value, x=0, core=0, z=0, y=0, where=None):
    pairs = []
    for place in np.ndindex(NX, NCORE, NZ, NY):
        if where is None or where(*place):
            a, b, c, d = place
            to = ((a + x) % NX, (b + core) % NCORE, (c + z) % NZ, (d + y) % NY)
            pairs.append((int(DEVICE[place]), int(DEVICE[to])))
    return lax.ppermute(value, AXES, pairs)


def pick(index, choices):
    value = choices[0]
    for number, choice in enumerate(choices[1:], 1):
        value = jnp.where(index == number, choice, value)
    return value


def per_device(matrix, pattern):
    tie = lambda *arrays: lax.optimization_barrier(arrays)
    p = lax.axis_index("row")
    q = lax.axis_index("col")
    x, core, z, y = (p // NCORE, p % NCORE, q // NY, q % NY)
    local = matrix.reshape(2, 4, 4 * BLK, HALF)
    head = matrix[0, 0, :, :, 0, :].transpose(1, 0, 2)
    quarters = head.transpose(0, 2, 1).reshape(4, HALF, BLK)

    parts = []
    for m in range(4):
        pairs = [(32 * c + s, (s % 8) * 32 + 8 * (s // 8) + 4 * c + m) for c in range(2) for s in range(32)]
        parts.append(lax.ppermute(quarters[m], AXES, pairs))
    mine = parts[0] + parts[1] + parts[2] + parts[3]
    mine, own = tie(mine, head[0])

    roots = ((0, 0, 0, 0), (0, 0, 0, 1), (0, 1, 0, 1))
    root = (x == 0) & (z == 0) & ((core == 0) & (y == 0) | (y == 1))
    g = jnp.stack([mine] + [shifted(mine, y=k) for k in (1, 2, 3)])
    along = [shifted(own, z=k, where=lambda *a: a in roots) for k in (2, 6, 4)]
    pivot = jnp.where(root, own, 0.0) + along[0] + along[1] + along[2]
    g, pivot = tie(g, pivot)

    groups = [[NY * b + a for b in range(NZ)] for a in range(NY)]
    g = lax.all_gather(g, "col", axis=0, axis_index_groups=groups)
    carries = lambda a, b, c, d: a == 0 and (d == 1 or (b == 0 and d == 0))
    pivot = pivot + shifted(pivot, z=1, where=lambda a, b, c, d: carries(a, b, c, d) and c % 2 == 0)
    got = [pivot] + [shifted(pivot, y=k, where=carries) for k in (1, 2, 3)]
    a00, rest = tie(pick(y, got), pick((y + 3) % 4, got))
    got = [a00] + [shifted(a00, x=k, where=lambda a, b, *_: a == 0 and b == 0) for k in (1, 2, 3)]
    a00, rest = tie(pick(x, got), rest)
    a00 = jnp.where(core == 0, a00, shifted(a00, core=1, where=lambda a, b, *_: b == 0))
    rest = pick(x, [rest] + [shifted(rest, x=k, where=lambda a, *_: a == 0) for k in (1, 2, 3)])
    a00, head = tie(a00, head)

    cols = pick(x, [head] + [shifted(head, x=k, where=lambda a, *_: a == 0) for k in (1, 2, 3)])
    (inv00,) = on_blocks(first_kernel, 1, "factor_first", a00)
    inv00, rest = tie(inv00, rest)
    swapped = shifted(rest, core=1)
    a01 = jnp.where(core == 0, rest, swapped)
    a11 = jnp.where(core == 0, swapped, rest)
    u01, inv11 = on_blocks(second_kernel, 2, "factor_second", inv00, a01, a11)
    u01, inv11, cols = tie(u01, inv11, cols)
    other = shifted(cols, core=1)
    ids = jnp.stack([p, q, core, y]).astype(jnp.int32)
    solved = solve_columns(ids, pattern, cols, other, inv00, u01, inv11)
    solved, g = tie(solved, g)
    out = update(ids, pattern, local, g, *solved)
    return out.reshape(matrix.shape)


def solution(mesh):
    return jax.shard_map(
        per_device,
        mesh=mesh,
        in_specs=(P(None, "row", None, None, "col", None), P()),
        out_specs=P(None, "row", None, None, "col", None),
        check_vma=False,
    )
```

```python
import functools

import jax
import jax.numpy as jnp
import numpy as np
from jax import lax
from jax.experimental import pallas as pl
from jax.experimental.pallas import tpu as pltpu
from jax.sharding import PartitionSpec as P

AXES = ("row", "col")
NX, NCORE, NZ, NY = (4, 2, 8, 4)
BLK = 256
HALF = 128
STEP = 8
DEVICE = np.arange(NX * NCORE * NZ * NY).reshape(NX, NCORE, NZ, NY)
VMEM = pl.BlockSpec(memory_space=pltpu.VMEM)


def dot(a, b, contract=((1,), (0,))):
    return lax.dot_general(a, b, (contract, ((), ())), precision=lax.Precision.HIGHEST, preferred_element_type=jnp.float32)


def invert_factor(block):
    n = block.shape[0]
    lane = lax.broadcasted_iota(jnp.int32, (8, n), 1)
    sub = lax.broadcasted_iota(jnp.int32, (8, n), 0)
    rows = [block[8 * g : 8 * g + 8, :] for g in range(n // 8)]
    for first in range(0, n, STEP):
        top, at = divmod(first, 8)
        inside = (lane >= first) & (lane < first + STEP)
        low = range(top, n // 8)
        column = {
            g: [jnp.broadcast_to(rows[g][:, first + k : first + k + 1], (8, n)) for k in range(STEP)] for g in low
        }
        pivot = [
            [jnp.broadcast_to(column[top][k][at + i : at + i + 1, :], (8, n)) for k in range(i + 1)]
            for i in range(STEP)
        ]
        upper = [
            jnp.where(
                inside,
                (lane == first + k).astype(jnp.float32),
                jnp.broadcast_to(rows[top][at + k : at + k + 1, :], (8, n)),
            )
            for k in range(STEP)
        ]
        inverse = []
        for k in range(STEP):
            inverse.append(1.0 / pivot[k][k])
            for i in range(k + 1, STEP):
                ratio = pivot[i][k] * inverse[k]
                for m in range(k + 1, i + 1):
                    pivot[i][m] = pivot[i][m] - ratio * pivot[m][k]
                upper[i] = upper[i] - ratio * upper[k]
                for g in low:
                    column[g][i] = column[g][i] - ratio * column[g][k]
        scaled = [upper[k] * inverse[k] for k in range(STEP)]
        for g in low:
            left = jnp.where(inside, 0.0, rows[g])
            for k in range(STEP):
                left = left - column[g][k] * scaled[k]
            if g == top:
                done = rows[g]
                for k in range(STEP):
                    done = jnp.where(sub == at + k, upper[k] * lax.rsqrt(pivot[k][k]), done)
                left = jnp.where(sub >= at + STEP, left, done)
            rows[g] = left
    whole = jnp.concatenate(rows, axis=0)
    r = lax.broadcasted_iota(jnp.int32, (n, n), 0)
    c = lax.broadcasted_iota(jnp.int32, (n, n), 1)
    return jnp.where(c <= r, whole, 0.0)


def invert_pair(block, out):
    h = HALF
    top = invert_factor(block[:h, :h])
    link = dot(top, block[:h, h:])
    low = invert_factor(block[h:, h:] - dot(link, link, ((0,), (0,))))
    out[:h, :h] = top
    out[:h, h:] = jnp.zeros((h, h), jnp.float32)
    out[h:, :h] = -dot(dot(low, link, ((1,), (1,))), top)
    out[h:, h:] = low


def pivots_kernel(a00, a01, a11, inv00, u01, inv11):
    invert_pair(a00[...], inv00)
    link = dot(inv00[...], a01[...])
    u01[...] = link
    invert_pair(a11[...] - dot(link, link, ((0,), (0,))), inv11)


def factor_pivots(a00, a01, a11):
    shape = jax.ShapeDtypeStruct((BLK, BLK), jnp.float32)
    return pl.pallas_call(
        pivots_kernel,
        out_shape=(shape, shape, shape),
        in_specs=[VMEM] * 3,
        out_specs=[VMEM] * 3,
        compiler_params=pltpu.CompilerParams(vmem_limit_bytes=32 << 20),
        cost_estimate=pl.CostEstimate(flops=25_000_000_000, bytes_accessed=1 << 20, transcendentals=0),
        name="factor_pivots",
    )(a00, a01, a11)


LEFT = {3: (0, 0, 1, 0, 1, 2), 2: (0, 1, 0)}
RIGHT = {3: (0, 1, 0, 2, 1, 0), 2: (0, 0, 1)}


def split(value, count=3):
    parts = []
    for number in range(count):
        parts.append(value.astype(jnp.bfloat16))
        if number + 1 < count:
            value = value - parts[-1].astype(jnp.float32)
    return parts


def product(left, right, count=3):
    a = jnp.concatenate([left[k] for k in LEFT[count]], axis=1)
    b = jnp.concatenate([right[k] for k in RIGHT[count]], axis=0)
    return jnp.dot(a, b, preferred_element_type=jnp.float32)


def columns_kernel(ids, pattern, y0, y1, inv00, u01, inv11, back0, back1, link, cols):
    for out, value in ((back0, inv00[...].T), (back1, inv11[...].T), (link, u01[...])):
        for number, part in enumerate(split(value)):
            out[number] = part
    q = ids[1]
    swap = ids[2] == 1
    inverse0, inverse1, down = (split(inv00[...]), split(inv11[...]), split(u01[...].T))
    for c in range(2):
        w = pattern[32 * c + q, 1].astype(jnp.float32)
        first = product(inverse0, split(jnp.where(swap, y1[c], y0[c])))
        left = jnp.where(swap, y0[c], y1[c]) - w * product(down, split(first))
        second = product(inverse1, split(left))
        for k, value in enumerate((first, second)):
            for number, part in enumerate(split(value, 2)):
                cols[c, number, k * BLK : (k + 1) * BLK, :] = part


def solve_columns(ids, pattern, y0, y1, inv00, u01, inv11):
    smem = pl.BlockSpec(memory_space=pltpu.SMEM)
    parts = jax.ShapeDtypeStruct((3, BLK, BLK), jnp.bfloat16)
    return pl.pallas_call(
        columns_kernel,
        out_shape=(parts, parts, parts, jax.ShapeDtypeStruct((2, 2, 2 * BLK, BLK), jnp.bfloat16)),
        in_specs=[smem, smem] + [VMEM] * 5,
        out_specs=[VMEM] * 4,
        compiler_params=pltpu.CompilerParams(vmem_limit_bytes=32 << 20),
        cost_estimate=pl.CostEstimate(flops=3_000_000_000, bytes_accessed=4 << 20, transcendentals=0),
        name="solve_columns",
    )(ids, pattern, y0, y1, inv00, u01, inv11)


def update_kernel(ids, pattern, local, g, back0, back1, link, cols, out):
    j = pl.program_id(0)
    p, q = (ids[0], ids[1])
    slots = [(ids[3] + 4 - m) % 4 for m in range(4)]
    raw = [jnp.concatenate([g[k, slot] for slot in slots], axis=0) for k in range(2)]
    first = product(split(raw[0]), back0)
    x0 = split(first)
    linked = product(x0, link)
    w = [pattern[(j + 4 * h) * 8 + p, 1].astype(jnp.float32) for h in range(2)]
    left = [raw[1][h * BLK : (h + 1) * BLK] - w[h] * linked[h * BLK : (h + 1) * BLK] for h in range(2)]
    second = product(split(jnp.concatenate(left, axis=0)), back1)
    x1 = split(second, 2)
    solved = [jnp.concatenate([x0[k], x1[k]], axis=1) for k in range(2)]
    for h in range(2):
        row_id = (j + 4 * h) * 8 + p
        rows = slice(h * BLK, (h + 1) * BLK)
        for c in range(2):
            col_id = 32 * c + q
            places = [pl.ds(2 * c + side, BLK, stride=4) for side in range(2)]
            halves = [slice(side * HALF, (side + 1) * HALF) for side in range(2)]
            panel = col_id < 2
            lower = row_id >= col_id
            changed = lower & ~panel & (pattern[row_id, col_id] != 0)

            @pl.when(panel)
            def _():
                r = lax.broadcasted_iota(jnp.int32, (BLK, BLK), 0)
                s = lax.broadcasted_iota(jnp.int32, (BLK, BLK), 1)
                kept = (row_id > col_id) | ((row_id == col_id) & (s <= r))
                value = jnp.where(kept, jnp.where(col_id == 0, first[rows], second[rows]), 0.0)
                for side in range(2):
                    out[h, 0, places[side], :] = value[:, halves[side]]

            @pl.when(~panel & ~lower)
            def _():
                for side in range(2):
                    out[h, 0, places[side], :] = jnp.zeros((BLK, HALF), jnp.float32)

            @pl.when(changed)
            def _():
                change = product([part[rows] for part in solved], cols[c], 2)
                for side in range(2):
                    out[h, 0, places[side], :] = local[h, 0, places[side], :] - change[:, halves[side]]

            @pl.when(lower & ~panel & ~changed)
            def _():
                for side in range(2):
                    out[h, 0, places[side], :] = local[h, 0, places[side], :]


def update(ids, pattern, local, g, back0, back1, link, cols):
    whole = lambda *shape: pl.BlockSpec(shape, lambda j, *_: (0,) * len(shape))
    block = pl.BlockSpec((2, 1, 4 * BLK, HALF), lambda j, *_: (0, j, 0, 0))
    return pl.pallas_call(
        update_kernel,
        out_shape=jax.ShapeDtypeStruct(local.shape, jnp.float32),
        grid_spec=pltpu.PrefetchScalarGridSpec(
            num_scalar_prefetch=2,
            grid=(4,),
            in_specs=[
                block,
                pl.BlockSpec((2, 4, HALF, BLK), lambda j, *_: (j, 0, 0, 0)),
                *[whole(3, BLK, BLK)] * 3,
                whole(2, 2, 2 * BLK, BLK),
            ],
            out_specs=block,
        ),
        compiler_params=pltpu.CompilerParams(vmem_limit_bytes=60 << 20),
        cost_estimate=pl.CostEstimate(flops=12_000_000_000, bytes_accessed=14 << 20, transcendentals=0),
        name="update",
    )(ids, pattern, local, g, back0, back1, link, cols)


def shifted(value, x=0, core=0, z=0, y=0, where=None):
    pairs = []
    for place in np.ndindex(NX, NCORE, NZ, NY):
        if where is None or where(*place):
            a, b, c, d = place
            to = ((a + x) % NX, (b + core) % NCORE, (c + z) % NZ, (d + y) % NY)
            pairs.append((int(DEVICE[place]), int(DEVICE[to])))
    return lax.ppermute(value, AXES, pairs)


def pick(index, choices):
    value = choices[0]
    for number, choice in enumerate(choices[1:], 1):
        value = jnp.where(index == number, choice, value)
    return value


def per_device(matrix, pattern):
    tie = lambda *arrays: lax.optimization_barrier(arrays)
    p = lax.axis_index("row")
    q = lax.axis_index("col")
    x, core, z, y = (p // NCORE, p % NCORE, q // NY, q % NY)
    local = matrix.reshape(2, 4, 4 * BLK, HALF)
    head = matrix[0, 0, :, :, 0, :].transpose(1, 0, 2)
    quarters = head.transpose(0, 2, 1).reshape(4, HALF, BLK)

    own = head[0]
    starts = lambda b, d: d == 1 or (b == 0 and d == 0)
    carrier = (y == 1) | ((core == 0) & (y == 0))
    along = [shifted(own, x=k, where=lambda a, b, c, d: a == 0 and c == 0 and starts(b, d)) for k in (1, 3, 2)]
    parts = []
    for m in range(4):
        pairs = [(32 * c + s, (s % 8) * 32 + 8 * (s // 8) + 4 * c + m) for c in range(2) for s in range(32)]
        parts.append(lax.ppermute(quarters[m], AXES, pairs))
    pivot = jnp.where((x == 0) & (z == 0) & carrier, own, 0.0) + along[0] + along[1] + along[2]
    along = [shifted(pivot, z=k, where=lambda a, b, c, d: c == 0 and starts(b, d)) for k in (2, 6, 4)]
    pivot = pivot + along[0] + along[1] + along[2]
    mine = parts[0] + parts[1] + parts[2] + parts[3]
    mine, pivot = tie(mine, pivot)

    g = jnp.stack([mine] + [shifted(mine, y=k) for k in (1, 2, 3)])
    pivot = pivot + shifted(pivot, z=1, where=lambda a, b, c, d: c % 2 == 0 and starts(b, d))
    g, pivot = tie(g, pivot)

    groups = [[NY * b + a for b in range(NZ)] for a in range(NY)]
    g = lax.all_gather(g, "col", axis=0, axis_index_groups=groups)
    got = [pivot] + [shifted(pivot, y=k, where=lambda a, b, c, d: starts(b, d)) for k in (1, 2, 3)]
    first = pick(y, got)
    rest = pick((y + 3) % 4, got)
    swapped = shifted(rest, core=1)
    a00 = jnp.where(core == 0, first, shifted(first, core=1, where=lambda a, b, *_: b == 0))
    a01 = jnp.where(core == 0, rest, swapped)
    a11 = jnp.where(core == 0, swapped, rest)
    a00, a01, a11, head = tie(a00, a01, a11, head)

    cols = [head] + [shifted(head, x=k, where=lambda a, *_: a == 0) for k in (1, 2, 3)]
    inv00, u01, inv11 = factor_pivots(a00, a01, a11)
    inv00, u01, inv11, cols[0] = tie(inv00, u01, inv11, cols[0])
    cols = pick(x, cols)
    other = shifted(cols, core=1)
    ids = jnp.stack([p, q, core, y]).astype(jnp.int32)
    solved = solve_columns(ids, pattern, cols, other, inv00, u01, inv11)
    solved, g = tie(solved, g)
    out = update(ids, pattern, local, g, *solved)
    return out.reshape(matrix.shape)


def solution(mesh):
    return jax.shard_map(
        per_device,
        mesh=mesh,
        in_specs=(P(None, "row", None, None, "col", None), P()),
        out_specs=P(None, "row", None, None, "col", None),
        check_vma=False,
    )
```

```python
import functools

import jax
import jax.numpy as jnp
import numpy as np
from jax import lax
from jax.experimental import pallas as pl
from jax.experimental.pallas import tpu as pltpu
from jax.sharding import PartitionSpec as P

AXES = ("row", "col")
NX, NCORE, NZ, NY = (4, 2, 8, 4)
BLK = 256
HALF = 128
STEP = 8
DEVICE = np.arange(NX * NCORE * NZ * NY).reshape(NX, NCORE, NZ, NY)
VMEM = pl.BlockSpec(memory_space=pltpu.VMEM)


LEFT = {3: (0, 0, 1, 0, 1, 2), 2: (0, 1, 0)}
RIGHT = {3: (0, 1, 0, 2, 1, 0), 2: (0, 0, 1)}


def split(value, count=3):
    parts = []
    for number in range(count):
        parts.append(value.astype(jnp.bfloat16))
        if number + 1 < count:
            value = value - parts[-1].astype(jnp.float32)
    return parts


def product(left, right, count=3):
    a = jnp.concatenate([left[k] for k in LEFT[count]], axis=1)
    b = jnp.concatenate([right[k] for k in RIGHT[count]], axis=0)
    return jnp.dot(a, b, preferred_element_type=jnp.float32)


def dot(a, b):
    return product(split(a), split(b))


def invert_factor(block):
    n = block.shape[0]
    lane = lax.broadcasted_iota(jnp.int32, (8, n), 1)
    sub = lax.broadcasted_iota(jnp.int32, (8, n), 0)
    rows = [block[8 * g : 8 * g + 8, :] for g in range(n // 8)]
    for first in range(0, n, STEP):
        top, at = divmod(first, 8)
        inside = (lane >= first) & (lane < first + STEP)
        low = range(top, n // 8)
        column = {
            g: [jnp.broadcast_to(rows[g][:, first + k : first + k + 1], (8, n)) for k in range(STEP)] for g in low
        }
        pivot = [
            [jnp.broadcast_to(column[top][k][at + i : at + i + 1, :], (8, n)) for k in range(i + 1)]
            for i in range(STEP)
        ]
        upper = [
            jnp.where(
                inside,
                (lane == first + k).astype(jnp.float32),
                jnp.broadcast_to(rows[top][at + k : at + k + 1, :], (8, n)),
            )
            for k in range(STEP)
        ]
        inverse = []
        for k in range(STEP):
            inverse.append(1.0 / pivot[k][k])
            for i in range(k + 1, STEP):
                ratio = pivot[i][k] * inverse[k]
                for m in range(k + 1, i + 1):
                    pivot[i][m] = pivot[i][m] - ratio * pivot[m][k]
                upper[i] = upper[i] - ratio * upper[k]
                for g in low:
                    column[g][i] = column[g][i] - ratio * column[g][k]
        scaled = [upper[k] * inverse[k] for k in range(STEP)]
        for g in low:
            left = jnp.where(inside, 0.0, rows[g])
            for k in range(STEP):
                left = left - column[g][k] * scaled[k]
            if g == top:
                done = rows[g]
                for k in range(STEP):
                    done = jnp.where(sub == at + k, upper[k] * lax.rsqrt(pivot[k][k]), done)
                left = jnp.where(sub >= at + STEP, left, done)
            rows[g] = left
    whole = jnp.concatenate(rows, axis=0)
    r = lax.broadcasted_iota(jnp.int32, (n, n), 0)
    c = lax.broadcasted_iota(jnp.int32, (n, n), 1)
    return jnp.where(c <= r, whole, 0.0)


def invert_pair(block, out):
    h = HALF
    top = invert_factor(block[:h, :h])
    link = dot(top, block[:h, h:])
    low = invert_factor(block[h:, h:] - dot(link.T, link))
    out[:h, :h] = top
    out[:h, h:] = jnp.zeros((h, h), jnp.float32)
    out[h:, :h] = -dot(dot(low, link.T), top)
    out[h:, h:] = low


def pivots_kernel(a00, a01, a11, inv00, u01, inv11):
    invert_pair(a00[...], inv00)
    link = dot(inv00[...], a01[...])
    u01[...] = link
    invert_pair(a11[...] - dot(link.T, link), inv11)


def factor_pivots(a00, a01, a11):
    shape = jax.ShapeDtypeStruct((BLK, BLK), jnp.float32)
    return pl.pallas_call(
        pivots_kernel,
        out_shape=(shape, shape, shape),
        in_specs=[VMEM] * 3,
        out_specs=[VMEM] * 3,
        compiler_params=pltpu.CompilerParams(vmem_limit_bytes=32 << 20),
        cost_estimate=pl.CostEstimate(flops=25_000_000_000, bytes_accessed=1 << 20, transcendentals=0),
        name="factor_pivots",
    )(a00, a01, a11)


def columns_kernel(ids, pattern, y0, y1, inv00, u01, inv11, back0, back1, link, cols):
    for out, value in ((back0, inv00[...].T), (back1, inv11[...].T), (link, u01[...])):
        for number, part in enumerate(split(value, 2)):
            out[number] = part
    q = ids[1]
    swap = ids[2] == 1
    inverse0, inverse1, down = (split(inv00[...]), split(inv11[...]), split(u01[...].T))
    for c in range(2):
        w = pattern[32 * c + q, 1].astype(jnp.float32)
        first = product(inverse0, split(jnp.where(swap, y1[c], y0[c])))
        left = jnp.where(swap, y0[c], y1[c]) - w * product(down, split(first))
        second = product(inverse1, split(left))
        for k, value in enumerate((first, second)):
            for number, part in enumerate(split(value, 2)):
                cols[c, number, k * BLK : (k + 1) * BLK, :] = part


def solve_columns(ids, pattern, y0, y1, inv00, u01, inv11):
    smem = pl.BlockSpec(memory_space=pltpu.SMEM)
    parts = jax.ShapeDtypeStruct((2, BLK, BLK), jnp.bfloat16)
    return pl.pallas_call(
        columns_kernel,
        out_shape=(parts, parts, parts, jax.ShapeDtypeStruct((2, 2, 2 * BLK, BLK), jnp.bfloat16)),
        in_specs=[smem, smem] + [VMEM] * 5,
        out_specs=[VMEM] * 4,
        compiler_params=pltpu.CompilerParams(vmem_limit_bytes=32 << 20),
        cost_estimate=pl.CostEstimate(flops=3_000_000_000, bytes_accessed=4 << 20, transcendentals=0),
        name="solve_columns",
    )(ids, pattern, y0, y1, inv00, u01, inv11)


def update_kernel(ids, pattern, local, g, back0, back1, link, cols, out):
    j = pl.program_id(0)
    p, q = (ids[0], ids[1])
    slots = [(ids[3] + 4 - m) % 4 for m in range(4)]
    raw = [jnp.concatenate([g[k, slot] for slot in slots], axis=0) for k in range(2)]
    first = product(split(raw[0], 2), back0, 2)
    x0 = split(first, 2)
    linked = product(x0, link, 2)
    w = [pattern[(j + 4 * h) * 8 + p, 1].astype(jnp.float32) for h in range(2)]
    left = [raw[1][h * BLK : (h + 1) * BLK] - w[h] * linked[h * BLK : (h + 1) * BLK] for h in range(2)]
    second = product(split(jnp.concatenate(left, axis=0), 2), back1, 2)
    x1 = split(second, 2)
    solved = [jnp.concatenate([x0[k], x1[k]], axis=1) for k in range(2)]
    for h in range(2):
        row_id = (j + 4 * h) * 8 + p
        rows = slice(h * BLK, (h + 1) * BLK)
        for c in range(2):
            col_id = 32 * c + q
            places = [pl.ds(2 * c + side, BLK, stride=4) for side in range(2)]
            halves = [slice(side * HALF, (side + 1) * HALF) for side in range(2)]
            panel = col_id < 2
            lower = row_id >= col_id
            changed = lower & ~panel & (pattern[row_id, col_id] != 0)

            @pl.when(panel)
            def _():
                r = lax.broadcasted_iota(jnp.int32, (BLK, BLK), 0)
                s = lax.broadcasted_iota(jnp.int32, (BLK, BLK), 1)
                kept = (row_id > col_id) | ((row_id == col_id) & (s <= r))
                value = jnp.where(kept, jnp.where(col_id == 0, first[rows], second[rows]), 0.0)
                for side in range(2):
                    out[h, 0, places[side], :] = value[:, halves[side]]

            @pl.when(~panel & ~lower)
            def _():
                for side in range(2):
                    out[h, 0, places[side], :] = jnp.zeros((BLK, HALF), jnp.float32)

            @pl.when(changed)
            def _():
                change = product([part[rows] for part in solved], cols[c], 2)
                for side in range(2):
                    out[h, 0, places[side], :] = local[h, 0, places[side], :] - change[:, halves[side]]

            @pl.when(lower & ~panel & ~changed)
            def _():
                for side in range(2):
                    out[h, 0, places[side], :] = local[h, 0, places[side], :]


def update(ids, pattern, local, g, back0, back1, link, cols):
    whole = lambda *shape: pl.BlockSpec(shape, lambda j, *_: (0,) * len(shape))
    block = pl.BlockSpec((2, 1, 4 * BLK, HALF), lambda j, *_: (0, j, 0, 0))
    return pl.pallas_call(
        update_kernel,
        out_shape=jax.ShapeDtypeStruct(local.shape, jnp.float32),
        grid_spec=pltpu.PrefetchScalarGridSpec(
            num_scalar_prefetch=2,
            grid=(4,),
            in_specs=[
                block,
                pl.BlockSpec((2, 4, HALF, BLK), lambda j, *_: (j, 0, 0, 0)),
                *[whole(2, BLK, BLK)] * 3,
                whole(2, 2, 2 * BLK, BLK),
            ],
            out_specs=block,
        ),
        compiler_params=pltpu.CompilerParams(vmem_limit_bytes=50 << 20),
        cost_estimate=pl.CostEstimate(flops=12_000_000_000, bytes_accessed=14 << 20, transcendentals=0),
        name="update",
    )(ids, pattern, local, g, back0, back1, link, cols)


def shifted(value, x=0, core=0, z=0, y=0, where=None):
    pairs = []
    for place in np.ndindex(NX, NCORE, NZ, NY):
        if where is None or where(*place):
            a, b, c, d = place
            to = ((a + x) % NX, (b + core) % NCORE, (c + z) % NZ, (d + y) % NY)
            pairs.append((int(DEVICE[place]), int(DEVICE[to])))
    return lax.ppermute(value, AXES, pairs)


def pick(index, choices):
    value = choices[0]
    for number, choice in enumerate(choices[1:], 1):
        value = jnp.where(index == number, choice, value)
    return value


def per_device(matrix, pattern):
    tie = lambda *arrays: lax.optimization_barrier(arrays)
    p = lax.axis_index("row")
    q = lax.axis_index("col")
    x, core, z, y = (p // NCORE, p % NCORE, q // NY, q % NY)
    local = matrix.reshape(2, 4, 4 * BLK, HALF)
    head = matrix[0, 0, :, :, 0, :].transpose(1, 0, 2)
    quarters = head.transpose(0, 2, 1).reshape(4, HALF, BLK)

    own = head[0]
    starts = lambda b, d: d == 1 or (b == 0 and d == 0)
    carrier = (y == 1) | ((core == 0) & (y == 0))
    parts = []
    for m in range(4):
        pairs = [(32 * c + s, (s % 8) * 32 + 8 * (s // 8) + 4 * c + m) for c in range(2) for s in range(32)]
        parts.append(lax.ppermute(quarters[m], AXES, pairs))
    along = [shifted(own, x=k, where=lambda a, b, c, d: a == 0 and c == 0 and starts(b, d)) for k in (1, 3, 2)]
    pivot = jnp.where((x == 0) & (z == 0) & carrier, own, 0.0) + along[0] + along[1] + along[2]
    mine = parts[0] + parts[1] + parts[2] + parts[3]
    mine, pivot = tie(mine, pivot)

    groups = [[NY * b + a for b in range(NZ)] for a in range(NY)]
    g = jnp.stack([mine] + [shifted(mine, y=k) for k in (1, 2, 3)])
    g = lax.all_gather(g, "col", axis=0, axis_index_groups=groups)
    along = [shifted(pivot, z=k, where=lambda a, b, c, d: c == 0 and starts(b, d)) for k in (2, 6, 4)]
    pivot = pivot + along[0] + along[1] + along[2]
    pivot = pivot + shifted(pivot, z=1, where=lambda a, b, c, d: c % 2 == 0 and starts(b, d))

    got = [pivot] + [shifted(pivot, y=k, where=lambda a, b, c, d: starts(b, d)) for k in (1, 2, 3)]
    first = pick(y, got)
    rest = pick((y + 3) % 4, got)
    swapped = shifted(rest, core=1)
    a00 = jnp.where(core == 0, first, shifted(first, core=1, where=lambda a, b, *_: b == 0))
    a01 = jnp.where(core == 0, rest, swapped)
    a11 = jnp.where(core == 0, swapped, rest)
    a00, a01, a11, head = tie(a00, a01, a11, head)

    cols = [head] + [shifted(head, x=k, where=lambda a, *_: a == 0) for k in (1, 2, 3)]
    inv00, u01, inv11 = factor_pivots(a00, a01, a11)
    inv00, u01, inv11, cols[0] = tie(inv00, u01, inv11, cols[0])
    cols = pick(x, cols)
    other = shifted(cols, core=1)
    ids = jnp.stack([p, q, core, y]).astype(jnp.int32)
    solved = solve_columns(ids, pattern, cols, other, inv00, u01, inv11)
    solved, g = tie(solved, g)
    out = update(ids, pattern, local, g, *solved)
    return out.reshape(matrix.shape)


def solution(mesh):
    return jax.shard_map(
        per_device,
        mesh=mesh,
        in_specs=(P(None, "row", None, None, "col", None), P()),
        out_specs=P(None, "row", None, None, "col", None),
        check_vma=False,
    )
```

```python
import functools

import jax
import jax.numpy as jnp
import numpy as np
from jax import lax
from jax.experimental import pallas as pl
from jax.experimental.pallas import tpu as pltpu
from jax.sharding import PartitionSpec as P

AXES = ("row", "col")
NX, NCORE, NZ, NY = (4, 2, 8, 4)
BLK = 256
HALF = 128
STEP = 8
DEVICE = np.arange(NX * NCORE * NZ * NY).reshape(NX, NCORE, NZ, NY)
VMEM = pl.BlockSpec(memory_space=pltpu.VMEM)


LEFT = {3: (0, 0, 1, 0, 1, 2), 2: (0, 1, 0)}
RIGHT = {3: (0, 1, 0, 2, 1, 0), 2: (0, 0, 1)}


def split(value, count=3):
    parts = []
    for number in range(count):
        parts.append(value.astype(jnp.bfloat16))
        if number + 1 < count:
            value = value - parts[-1].astype(jnp.float32)
    return parts


def product(left, right, count=3):
    a = jnp.concatenate([left[k] for k in LEFT[count]], axis=1)
    b = jnp.concatenate([right[k] for k in RIGHT[count]], axis=0)
    return jnp.dot(a, b, preferred_element_type=jnp.float32)


def dot(a, b):
    return product(split(a), split(b))


def invert_factor(block):
    n = block.shape[0]
    lane = lax.broadcasted_iota(jnp.int32, (8, n), 1)
    sub = lax.broadcasted_iota(jnp.int32, (8, n), 0)
    rows = [block[8 * g : 8 * g + 8, :] for g in range(n // 8)]
    for first in range(0, n, STEP):
        top, at = divmod(first, 8)
        inside = (lane >= first) & (lane < first + STEP)
        low = range(top, n // 8)
        column = {
            g: [jnp.broadcast_to(rows[g][:, first + k : first + k + 1], (8, n)) for k in range(STEP)] for g in low
        }
        pivot = [
            [jnp.broadcast_to(column[top][k][at + i : at + i + 1, :], (8, n)) for k in range(i + 1)]
            for i in range(STEP)
        ]
        upper = [
            jnp.where(
                inside,
                (lane == first + k).astype(jnp.float32),
                jnp.broadcast_to(rows[top][at + k : at + k + 1, :], (8, n)),
            )
            for k in range(STEP)
        ]
        inverse = []
        for k in range(STEP):
            inverse.append(1.0 / pivot[k][k])
            for i in range(k + 1, STEP):
                ratio = pivot[i][k] * inverse[k]
                for m in range(k + 1, i + 1):
                    pivot[i][m] = pivot[i][m] - ratio * pivot[m][k]
                upper[i] = upper[i] - ratio * upper[k]
                for g in low:
                    column[g][i] = column[g][i] - ratio * column[g][k]
        scaled = [upper[k] * inverse[k] for k in range(STEP)]
        for g in low:
            left = jnp.where(inside, 0.0, rows[g])
            for k in range(STEP):
                left = left - column[g][k] * scaled[k]
            if g == top:
                done = rows[g]
                for k in range(STEP):
                    done = jnp.where(sub == at + k, upper[k] * lax.rsqrt(pivot[k][k]), done)
                left = jnp.where(sub >= at + STEP, left, done)
            rows[g] = left
    whole = jnp.concatenate(rows, axis=0)
    r = lax.broadcasted_iota(jnp.int32, (n, n), 0)
    c = lax.broadcasted_iota(jnp.int32, (n, n), 1)
    return jnp.where(c <= r, whole, 0.0)


def invert_pair(block, out):
    h = HALF
    top = invert_factor(block[:h, :h])
    link = dot(top, block[:h, h:])
    low = invert_factor(block[h:, h:] - dot(link.T, link))
    out[:h, :h] = top
    out[:h, h:] = jnp.zeros((h, h), jnp.float32)
    out[h:, :h] = -dot(dot(low, link.T), top)
    out[h:, h:] = low


def pivots_kernel(a00, a01, a11, inv00, u01, inv11):
    invert_pair(a00[...], inv00)
    link = dot(inv00[...], a01[...])
    u01[...] = link
    invert_pair(a11[...] - dot(link.T, link), inv11)


def factor_pivots(a00, a01, a11):
    shape = jax.ShapeDtypeStruct((BLK, BLK), jnp.float32)
    return pl.pallas_call(
        pivots_kernel,
        out_shape=(shape, shape, shape),
        in_specs=[VMEM] * 3,
        out_specs=[VMEM] * 3,
        compiler_params=pltpu.CompilerParams(vmem_limit_bytes=32 << 20),
        cost_estimate=pl.CostEstimate(flops=25_000_000_000, bytes_accessed=1 << 20, transcendentals=0),
        name="factor_pivots",
    )(a00, a01, a11)


def columns_kernel(ids, pattern, y0, y1, inv00, u01, inv11, back0, back1, link, cols):
    for out, value in ((back0, inv00[...].T), (back1, inv11[...].T), (link, u01[...])):
        for number, part in enumerate(split(value, 2)):
            out[number] = part
    q = ids[1]
    swap = ids[2] == 1
    inverse0, inverse1, down = (split(inv00[...]), split(inv11[...]), split(u01[...].T))
    for c in range(2):
        w = pattern[32 * c + q, 1].astype(jnp.float32)
        first = product(inverse0, split(jnp.where(swap, y1[c], y0[c])))
        left = jnp.where(swap, y0[c], y1[c]) - w * product(down, split(first))
        second = product(inverse1, split(left))
        for k, value in enumerate((first, second)):
            for number, part in enumerate(split(value, 2)):
                cols[c, number, k * BLK : (k + 1) * BLK, :] = part


def solve_columns(ids, pattern, y0, y1, inv00, u01, inv11):
    smem = pl.BlockSpec(memory_space=pltpu.SMEM)
    parts = jax.ShapeDtypeStruct((2, BLK, BLK), jnp.bfloat16)
    return pl.pallas_call(
        columns_kernel,
        out_shape=(parts, parts, parts, jax.ShapeDtypeStruct((2, 2, 2 * BLK, BLK), jnp.bfloat16)),
        in_specs=[smem, smem] + [VMEM] * 5,
        out_specs=[VMEM] * 4,
        compiler_params=pltpu.CompilerParams(vmem_limit_bytes=32 << 20),
        cost_estimate=pl.CostEstimate(flops=3_000_000_000, bytes_accessed=4 << 20, transcendentals=0),
        name="solve_columns",
    )(ids, pattern, y0, y1, inv00, u01, inv11)


def update_kernel(ids, pattern, local, g, back0, back1, link, cols, out):
    j = pl.program_id(0)
    p, q = (ids[0], ids[1])
    slots = [(ids[3] + 4 - m) % 4 for m in range(4)]
    raw = [jnp.concatenate([g[k, slot] for slot in slots], axis=0) for k in range(2)]
    first = product(split(raw[0], 2), back0, 2)
    x0 = split(first, 2)
    linked = product(x0, link, 2)
    w = [pattern[(j + 4 * h) * 8 + p, 1].astype(jnp.float32) for h in range(2)]
    left = [raw[1][h * BLK : (h + 1) * BLK] - w[h] * linked[h * BLK : (h + 1) * BLK] for h in range(2)]
    second = product(split(jnp.concatenate(left, axis=0), 2), back1, 2)
    x1 = split(second, 2)
    solved = [jnp.concatenate([x0[k], x1[k]], axis=1) for k in range(2)]
    for h in range(2):
        row_id = (j + 4 * h) * 8 + p
        rows = slice(h * BLK, (h + 1) * BLK)
        for c in range(2):
            col_id = 32 * c + q
            places = [pl.ds(2 * c + side, BLK, stride=4) for side in range(2)]
            halves = [slice(side * HALF, (side + 1) * HALF) for side in range(2)]
            panel = col_id < 2
            lower = row_id >= col_id
            changed = lower & ~panel & (pattern[row_id, col_id] != 0)

            @pl.when(panel)
            def _():
                r = lax.broadcasted_iota(jnp.int32, (BLK, BLK), 0)
                s = lax.broadcasted_iota(jnp.int32, (BLK, BLK), 1)
                kept = (row_id > col_id) | ((row_id == col_id) & (s <= r))
                value = jnp.where(kept, jnp.where(col_id == 0, first[rows], second[rows]), 0.0)
                for side in range(2):
                    out[h, 0, places[side], :] = value[:, halves[side]]

            @pl.when(~panel & ~lower)
            def _():
                for side in range(2):
                    out[h, 0, places[side], :] = jnp.zeros((BLK, HALF), jnp.float32)

            @pl.when(changed)
            def _():
                change = product([part[rows] for part in solved], cols[c], 2)
                for side in range(2):
                    out[h, 0, places[side], :] = local[h, 0, places[side], :] - change[:, halves[side]]

            @pl.when(lower & ~panel & ~changed)
            def _():
                for side in range(2):
                    out[h, 0, places[side], :] = local[h, 0, places[side], :]


def update(ids, pattern, local, g, back0, back1, link, cols):
    whole = lambda *shape: pl.BlockSpec(shape, lambda j, *_: (0,) * len(shape))
    block = pl.BlockSpec((2, 1, 4 * BLK, HALF), lambda j, *_: (0, j, 0, 0))
    return pl.pallas_call(
        update_kernel,
        out_shape=jax.ShapeDtypeStruct(local.shape, jnp.float32),
        grid_spec=pltpu.PrefetchScalarGridSpec(
            num_scalar_prefetch=2,
            grid=(4,),
            in_specs=[
                block,
                pl.BlockSpec((2, 4, HALF, BLK), lambda j, *_: (j, 0, 0, 0)),
                *[whole(2, BLK, BLK)] * 3,
                whole(2, 2, 2 * BLK, BLK),
            ],
            out_specs=block,
        ),
        compiler_params=pltpu.CompilerParams(vmem_limit_bytes=50 << 20),
        cost_estimate=pl.CostEstimate(flops=12_000_000_000, bytes_accessed=14 << 20, transcendentals=0),
        name="update",
    )(ids, pattern, local, g, back0, back1, link, cols)


def shifted(value, x=0, core=0, z=0, y=0, where=None):
    pairs = []
    for place in np.ndindex(NX, NCORE, NZ, NY):
        if where is None or where(*place):
            a, b, c, d = place
            to = ((a + x) % NX, (b + core) % NCORE, (c + z) % NZ, (d + y) % NY)
            pairs.append((int(DEVICE[place]), int(DEVICE[to])))
    return lax.ppermute(value, AXES, pairs)


def pick(index, choices):
    value = choices[0]
    for number, choice in enumerate(choices[1:], 1):
        value = jnp.where(index == number, choice, value)
    return value


def per_device(matrix, pattern):
    tie = lambda *arrays: lax.optimization_barrier(arrays)
    p = lax.axis_index("row")
    q = lax.axis_index("col")
    x, core, z, y = (p // NCORE, p % NCORE, q // NY, q % NY)
    local = matrix.reshape(2, 4, 4 * BLK, HALF)
    head = matrix[0, 0, :, :, 0, :].transpose(1, 0, 2)
    quarters = head.transpose(0, 2, 1).reshape(4, HALF, BLK)

    own = head[0]
    starts = lambda b, d: d == 1 or (b == 0 and d == 0)
    carrier = (y == 1) | ((core == 0) & (y == 0))
    along = [shifted(own, z=k, where=lambda a, b, c, d: a == 0 and c == 0 and starts(b, d)) for k in (2, 6, 4)]
    parts = []
    for m in range(4):
        pairs = [(32 * c + s, (s % 8) * 32 + 8 * (s // 8) + 4 * c + m) for c in range(2) for s in range(32)]
        parts.append(lax.ppermute(quarters[m], AXES, pairs))
    pivot = jnp.where((x == 0) & (z == 0) & carrier, own, 0.0) + along[0] + along[1] + along[2]
    pivot = pivot + shifted(pivot, z=1, where=lambda a, b, c, d: a == 0 and c % 2 == 0 and starts(b, d))
    mine = parts[0] + parts[1] + parts[2] + parts[3]
    mine, pivot = tie(mine, pivot)

    groups = [[NY * b + a for b in range(NZ)] for a in range(NY)]
    g = jnp.stack([mine] + [shifted(mine, y=k) for k in (1, 2, 3)])
    g = lax.all_gather(g, "col", axis=0, axis_index_groups=groups)
    along = [shifted(pivot, x=k, where=lambda a, b, c, d: a == 0 and starts(b, d)) for k in (1, 3, 2)]
    pivot = pivot + along[0] + along[1] + along[2]
    got = [pivot] + [shifted(pivot, y=k, where=lambda a, b, c, d: starts(b, d)) for k in (1, 2, 3)]
    first = pick(y, got)
    rest = pick((y + 3) % 4, got)
    swapped = shifted(rest, core=1)
    a00 = jnp.where(core == 0, first, shifted(first, core=1, where=lambda a, b, *_: b == 0))
    a01 = jnp.where(core == 0, rest, swapped)
    a11 = jnp.where(core == 0, swapped, rest)
    a00, a01, a11, head = tie(a00, a01, a11, head)

    cols = [head] + [shifted(head, x=k, where=lambda a, *_: a == 0) for k in (1, 2, 3)]
    inv00, u01, inv11 = factor_pivots(a00, a01, a11)
    inv00, u01, inv11, cols[0] = tie(inv00, u01, inv11, cols[0])
    cols = pick(x, cols)
    other = shifted(cols, core=1)
    ids = jnp.stack([p, q, core, y]).astype(jnp.int32)
    solved = solve_columns(ids, pattern, cols, other, inv00, u01, inv11)
    solved, g = tie(solved, g)
    out = update(ids, pattern, local, g, *solved)
    return out.reshape(matrix.shape)


def solution(mesh):
    return jax.shard_map(
        per_device,
        mesh=mesh,
        in_specs=(P(None, "row", None, None, "col", None), P()),
        out_specs=P(None, "row", None, None, "col", None),
        check_vma=False,
    )
```

```python
import functools

import jax
import jax.numpy as jnp
import numpy as np
from jax import lax
from jax.experimental import pallas as pl
from jax.experimental.pallas import tpu as pltpu
from jax.sharding import PartitionSpec as P

AXES = ("row", "col")
NX, NCORE, NZ, NY = (4, 2, 8, 4)
BLK = 256
HALF = 128
STEP = 8
DEVICE = np.arange(NX * NCORE * NZ * NY).reshape(NX, NCORE, NZ, NY)
VMEM = pl.BlockSpec(memory_space=pltpu.VMEM)


LEFT = {3: (0, 0, 1, 0, 1, 2), 2: (0, 1, 0)}
RIGHT = {3: (0, 1, 0, 2, 1, 0), 2: (0, 0, 1)}


def split(value, count=3):
    parts = []
    for number in range(count):
        parts.append(value.astype(jnp.bfloat16))
        if number + 1 < count:
            value = value - parts[-1].astype(jnp.float32)
    return parts


def product(left, right, count=3):
    a = jnp.concatenate([left[k] for k in LEFT[count]], axis=1)
    b = jnp.concatenate([right[k] for k in RIGHT[count]], axis=0)
    return jnp.dot(a, b, preferred_element_type=jnp.float32)


def dot(a, b):
    return product(split(a), split(b))


def invert_factor(block):
    n = block.shape[0]
    lane = lax.broadcasted_iota(jnp.int32, (8, n), 1)
    sub = lax.broadcasted_iota(jnp.int32, (8, n), 0)
    rows = [block[8 * g : 8 * g + 8, :] for g in range(n // 8)]
    for first in range(0, n, STEP):
        top, at = divmod(first, 8)
        inside = (lane >= first) & (lane < first + STEP)
        low = range(top, n // 8)
        column = {
            g: [jnp.broadcast_to(rows[g][:, first + k : first + k + 1], (8, n)) for k in range(STEP)] for g in low
        }
        pivot = [
            [jnp.broadcast_to(column[top][k][at + i : at + i + 1, :], (8, n)) for k in range(i + 1)]
            for i in range(STEP)
        ]
        upper = [
            jnp.where(
                inside,
                (lane == first + k).astype(jnp.float32),
                jnp.broadcast_to(rows[top][at + k : at + k + 1, :], (8, n)),
            )
            for k in range(STEP)
        ]
        inverse = []
        for k in range(STEP):
            inverse.append(1.0 / pivot[k][k])
            for i in range(k + 1, STEP):
                ratio = pivot[i][k] * inverse[k]
                for m in range(k + 1, i + 1):
                    pivot[i][m] = pivot[i][m] - ratio * pivot[m][k]
                upper[i] = upper[i] - ratio * upper[k]
                for g in low:
                    column[g][i] = column[g][i] - ratio * column[g][k]
        scaled = [upper[k] * inverse[k] for k in range(STEP)]
        for g in low:
            left = jnp.where(inside, 0.0, rows[g])
            for k in range(STEP):
                left = left - column[g][k] * scaled[k]
            if g == top:
                done = rows[g]
                for k in range(STEP):
                    done = jnp.where(sub == at + k, upper[k] * lax.rsqrt(pivot[k][k]), done)
                left = jnp.where(sub >= at + STEP, left, done)
            rows[g] = left
    whole = jnp.concatenate(rows, axis=0)
    r = lax.broadcasted_iota(jnp.int32, (n, n), 0)
    c = lax.broadcasted_iota(jnp.int32, (n, n), 1)
    return jnp.where(c <= r, whole, 0.0)


def invert_pair(blocks, out):
    h = HALF
    top = invert_factor(blocks[0])
    link = dot(top, blocks[1])
    low = invert_factor(blocks[2] - dot(link.T, link))
    out[:h, :h] = top
    out[:h, h:] = jnp.zeros((h, h), jnp.float32)
    out[h:, :h] = -dot(dot(low, link.T), top)
    out[h:, h:] = low


def pivots_kernel(even, odd, inv00, u01, inv11):
    h = HALF
    invert_pair([even[0, k] for k in range(3)], inv00)
    upper = jnp.concatenate([even[1, 0], even[1, 1]], axis=1)
    lower = jnp.concatenate([odd[0, 1].T, odd[0, 2].T], axis=1)
    link = dot(inv00[...], jnp.concatenate([upper, lower], axis=0))
    u01[...] = link
    change = dot(link.T, link)
    parts = (change[:h, :h], change[:h, h:], change[h:, h:])
    invert_pair([odd[1, k] - parts[k] for k in range(3)], inv11)


def factor_pivots(even, odd):
    shape = jax.ShapeDtypeStruct((BLK, BLK), jnp.float32)
    return pl.pallas_call(
        pivots_kernel,
        out_shape=(shape, shape, shape),
        in_specs=[VMEM] * 2,
        out_specs=[VMEM] * 3,
        compiler_params=pltpu.CompilerParams(vmem_limit_bytes=32 << 20),
        cost_estimate=pl.CostEstimate(flops=25_000_000_000, bytes_accessed=1 << 20, transcendentals=0),
        name="factor_pivots",
    )(even, odd)


def columns_kernel(ids, pattern, y0, y1, inv00, u01, inv11, back0, back1, link, cols):
    for out, value in ((back0, inv00[...].T), (back1, inv11[...].T), (link, u01[...])):
        for number, part in enumerate(split(value, 2)):
            out[number] = part
    q = ids[1]
    swap = ids[2] == 1
    inverse0, inverse1, down = (split(inv00[...], 2), split(inv11[...], 2), split(u01[...].T, 2))
    for c in range(2):
        w = pattern[32 * c + q, 1].astype(jnp.float32)
        first = product(inverse0, split(jnp.where(swap, y1[c], y0[c]), 2), 2)
        left = jnp.where(swap, y0[c], y1[c]) - w * product(down, split(first, 2), 2)
        second = product(inverse1, split(left, 2), 2)
        for k, value in enumerate((first, second)):
            for number, part in enumerate(split(value, 2)):
                cols[c, number, k * BLK : (k + 1) * BLK, :] = part


def solve_columns(ids, pattern, y0, y1, inv00, u01, inv11):
    smem = pl.BlockSpec(memory_space=pltpu.SMEM)
    parts = jax.ShapeDtypeStruct((2, BLK, BLK), jnp.bfloat16)
    return pl.pallas_call(
        columns_kernel,
        out_shape=(parts, parts, parts, jax.ShapeDtypeStruct((2, 2, 2 * BLK, BLK), jnp.bfloat16)),
        in_specs=[smem, smem] + [VMEM] * 5,
        out_specs=[VMEM] * 4,
        compiler_params=pltpu.CompilerParams(vmem_limit_bytes=32 << 20),
        cost_estimate=pl.CostEstimate(flops=3_000_000_000, bytes_accessed=4 << 20, transcendentals=0),
        name="solve_columns",
    )(ids, pattern, y0, y1, inv00, u01, inv11)


def update_kernel(ids, pattern, local, g, back0, back1, link, cols, out):
    j = pl.program_id(0)
    p, q = (ids[0], ids[1])
    slots = [(ids[3] + 4 - m) % 4 for m in range(4)]
    raw = [jnp.concatenate([g[k, slot] for slot in slots], axis=0) for k in range(2)]
    first = product(split(raw[0], 2), back0, 2)
    x0 = split(first, 2)
    linked = product(x0, link, 2)
    w = [pattern[(j + 4 * h) * 8 + p, 1].astype(jnp.float32) for h in range(2)]
    left = [raw[1][h * BLK : (h + 1) * BLK] - w[h] * linked[h * BLK : (h + 1) * BLK] for h in range(2)]
    second = product(split(jnp.concatenate(left, axis=0), 2), back1, 2)
    x1 = split(second, 2)
    solved = [jnp.concatenate([x0[k], x1[k]], axis=1) for k in range(2)]
    for h in range(2):
        row_id = (j + 4 * h) * 8 + p
        rows = slice(h * BLK, (h + 1) * BLK)
        for c in range(2):
            col_id = 32 * c + q
            places = [pl.ds(2 * c + side, BLK, stride=4) for side in range(2)]
            halves = [slice(side * HALF, (side + 1) * HALF) for side in range(2)]
            panel = col_id < 2
            lower = row_id >= col_id
            changed = lower & ~panel & (pattern[row_id, col_id] != 0)

            @pl.when(panel)
            def _():
                r = lax.broadcasted_iota(jnp.int32, (BLK, BLK), 0)
                s = lax.broadcasted_iota(jnp.int32, (BLK, BLK), 1)
                kept = (row_id > col_id) | ((row_id == col_id) & (s <= r))
                value = jnp.where(kept, jnp.where(col_id == 0, first[rows], second[rows]), 0.0)
                for side in range(2):
                    out[h, 0, places[side], :] = value[:, halves[side]]

            @pl.when(~panel & ~lower)
            def _():
                for side in range(2):
                    out[h, 0, places[side], :] = jnp.zeros((BLK, HALF), jnp.float32)

            @pl.when(changed)
            def _():
                change = product([part[rows] for part in solved], cols[c], 2)
                for side in range(2):
                    out[h, 0, places[side], :] = local[h, 0, places[side], :] - change[:, halves[side]]

            @pl.when(lower & ~panel & ~changed)
            def _():
                for side in range(2):
                    out[h, 0, places[side], :] = local[h, 0, places[side], :]


def update(ids, pattern, local, g, back0, back1, link, cols):
    whole = lambda *shape: pl.BlockSpec(shape, lambda j, *_: (0,) * len(shape))
    block = pl.BlockSpec((2, 1, 4 * BLK, HALF), lambda j, *_: (0, j, 0, 0))
    return pl.pallas_call(
        update_kernel,
        out_shape=jax.ShapeDtypeStruct(local.shape, jnp.float32),
        grid_spec=pltpu.PrefetchScalarGridSpec(
            num_scalar_prefetch=2,
            grid=(4,),
            in_specs=[
                block,
                pl.BlockSpec((2, 4, HALF, BLK), lambda j, *_: (j, 0, 0, 0)),
                *[whole(2, BLK, BLK)] * 3,
                whole(2, 2, 2 * BLK, BLK),
            ],
            out_specs=block,
        ),
        compiler_params=pltpu.CompilerParams(vmem_limit_bytes=50 << 20),
        cost_estimate=pl.CostEstimate(flops=12_000_000_000, bytes_accessed=14 << 20, transcendentals=0),
        name="update",
    )(ids, pattern, local, g, back0, back1, link, cols)


def shifted(value, x=0, core=0, z=0, y=0, where=None):
    pairs = []
    for place in np.ndindex(NX, NCORE, NZ, NY):
        if where is None or where(*place):
            a, b, c, d = place
            to = ((a + x) % NX, (b + core) % NCORE, (c + z) % NZ, (d + y) % NY)
            pairs.append((int(DEVICE[place]), int(DEVICE[to])))
    return lax.ppermute(value, AXES, pairs)


def pick(index, choices):
    value = choices[0]
    for number, choice in enumerate(choices[1:], 1):
        value = jnp.where(index == number, choice, value)
    return value


def per_device(matrix, pattern):
    tie = lambda *arrays: lax.optimization_barrier(arrays)
    p = lax.axis_index("row")
    q = lax.axis_index("col")
    x, core, z, y = (p // NCORE, p % NCORE, q // NY, q % NY)
    local = matrix.reshape(2, 4, 4 * BLK, HALF)
    head = matrix[0, 0, :, :, 0, :].transpose(1, 0, 2)
    quarters = head.transpose(0, 2, 1).reshape(4, HALF, BLK)

    corner = head[0]
    own = jnp.stack([corner[:HALF, :HALF], corner[:HALF, HALF:], corner[HALF:, HALF:]])
    along = [shifted(own, x=k, where=lambda a, b, c, d: a == 0 and c == 0 and d < 2) for k in (1, 3, 2)]
    parts = []
    for m in range(4):
        pairs = [(32 * c + s, (s % 8) * 32 + 8 * (s // 8) + 4 * c + m) for c in range(2) for s in range(32)]
        parts.append(lax.ppermute(quarters[m], AXES, pairs))
    pivot = jnp.where((x == 0) & (z == 0) & (y < 2), own, 0.0) + along[0] + along[1] + along[2]
    along = [shifted(pivot, z=k, where=lambda a, b, c, d: c == 0 and d < 2) for k in (2, 6, 4)]
    pivot = pivot + along[0] + along[1] + along[2]
    mine = parts[0] + parts[1] + parts[2] + parts[3]
    mine, pivot = tie(mine, pivot)

    g = jnp.stack([mine] + [shifted(mine, y=k) for k in (1, 2, 3)])
    pivot = pivot + shifted(pivot, z=1, where=lambda a, b, c, d: c % 2 == 0 and d < 2)
    g, pivot = tie(g, pivot)

    groups = [[NY * b + a for b in range(NZ)] for a in range(NY)]
    g = lax.all_gather(g, "col", axis=0, axis_index_groups=groups)
    got = [pivot] + [shifted(pivot, y=k, where=lambda a, b, c, d: d < 2) for k in (1, 2, 3)]
    both = jnp.stack([pick(y, got), pick((y + 3) % 4, got)])
    swapped = shifted(both, core=1)
    even = jnp.where(core == 0, both, swapped)
    odd = jnp.where(core == 0, swapped, both)
    even, odd, head = tie(even, odd, head)

    cols = [head] + [shifted(head, x=k, where=lambda a, *_: a == 0) for k in (1, 2, 3)]
    inv00, u01, inv11 = factor_pivots(even, odd)
    inv00, u01, inv11, cols[0] = tie(inv00, u01, inv11, cols[0])
    cols = pick(x, cols)
    other = shifted(cols, core=1)
    ids = jnp.stack([p, q, core, y]).astype(jnp.int32)
    solved = solve_columns(ids, pattern, cols, other, inv00, u01, inv11)
    solved, g = tie(solved, g)
    out = update(ids, pattern, local, g, *solved)
    return out.reshape(matrix.shape)


def solution(mesh):
    return jax.shard_map(
        per_device,
        mesh=mesh,
        in_specs=(P(None, "row", None, None, "col", None), P()),
        out_specs=P(None, "row", None, None, "col", None),
        check_vma=False,
    )
```

```python
import functools

import jax
import jax.numpy as jnp
import numpy as np
from jax import lax
from jax.experimental import pallas as pl
from jax.experimental.pallas import tpu as pltpu
from jax.sharding import PartitionSpec as P

AXES = ("row", "col")
NX, NCORE, NZ, NY = (4, 2, 8, 4)
BLK = 256
HALF = 128
STEP = 8
DEVICE = np.arange(NX * NCORE * NZ * NY).reshape(NX, NCORE, NZ, NY)
VMEM = pl.BlockSpec(memory_space=pltpu.VMEM)


LEFT = {3: (0, 0, 1, 0, 1, 2), 2: (0, 1, 0)}
RIGHT = {3: (0, 1, 0, 2, 1, 0), 2: (0, 0, 1)}


def split(value, count=3):
    parts = []
    for number in range(count):
        parts.append(value.astype(jnp.bfloat16))
        if number + 1 < count:
            value = value - parts[-1].astype(jnp.float32)
    return parts


def product(left, right, count=3):
    a = jnp.concatenate([left[k] for k in LEFT[count]], axis=1)
    b = jnp.concatenate([right[k] for k in RIGHT[count]], axis=0)
    return jnp.dot(a, b, preferred_element_type=jnp.float32)


def dot(a, b):
    return product(split(a), split(b))


def invert_factor(block):
    n = block.shape[0]
    lane = lax.broadcasted_iota(jnp.int32, (8, n), 1)
    sub = lax.broadcasted_iota(jnp.int32, (8, n), 0)
    rows = [block[8 * g : 8 * g + 8, :] for g in range(n // 8)]
    for first in range(0, n, STEP):
        top, at = divmod(first, 8)
        inside = (lane >= first) & (lane < first + STEP)
        low = range(top, n // 8)
        column = {
            g: [jnp.broadcast_to(rows[g][:, first + k : first + k + 1], (8, n)) for k in range(STEP)] for g in low
        }
        pivot = [
            [jnp.broadcast_to(column[top][k][at + i : at + i + 1, :], (8, n)) for k in range(i + 1)]
            for i in range(STEP)
        ]
        upper = [
            jnp.where(
                inside,
                (lane == first + k).astype(jnp.float32),
                jnp.broadcast_to(rows[top][at + k : at + k + 1, :], (8, n)),
            )
            for k in range(STEP)
        ]
        inverse = []
        for k in range(STEP):
            inverse.append(1.0 / pivot[k][k])
            for i in range(k + 1, STEP):
                ratio = pivot[i][k] * inverse[k]
                for m in range(k + 1, i + 1):
                    pivot[i][m] = pivot[i][m] - ratio * pivot[m][k]
                upper[i] = upper[i] - ratio * upper[k]
                for g in low:
                    column[g][i] = column[g][i] - ratio * column[g][k]
        scaled = [upper[k] * inverse[k] for k in range(STEP)]
        for g in low:
            left = jnp.where(inside, 0.0, rows[g])
            for k in range(STEP):
                left = left - column[g][k] * scaled[k]
            if g == top:
                done = rows[g]
                for k in range(STEP):
                    done = jnp.where(sub == at + k, upper[k] * lax.rsqrt(pivot[k][k]), done)
                left = jnp.where(sub >= at + STEP, left, done)
            rows[g] = left
    whole = jnp.concatenate(rows, axis=0)
    r = lax.broadcasted_iota(jnp.int32, (n, n), 0)
    c = lax.broadcasted_iota(jnp.int32, (n, n), 1)
    return jnp.where(c <= r, whole, 0.0)


def invert_pair(blocks, out):
    h = HALF
    top = invert_factor(blocks[0])
    link = dot(top, blocks[1])
    low = invert_factor(blocks[2] - dot(link.T, link))
    out[:h, :h] = top
    out[:h, h:] = jnp.zeros((h, h), jnp.float32)
    out[h:, :h] = -dot(dot(low, link.T), top)
    out[h:, h:] = low


def pivots_kernel(even, odd, inv00, u01, inv11):
    h = HALF
    invert_pair([even[0, k] for k in range(3)], inv00)
    upper = jnp.concatenate([even[1, 0], even[1, 1]], axis=1)
    lower = jnp.concatenate([odd[0, 1].T, odd[0, 2].T], axis=1)
    link = dot(inv00[...], jnp.concatenate([upper, lower], axis=0))
    u01[...] = link
    change = dot(link.T, link)
    parts = (change[:h, :h], change[:h, h:], change[h:, h:])
    invert_pair([odd[1, k] - parts[k] for k in range(3)], inv11)


def factor_pivots(even, odd):
    shape = jax.ShapeDtypeStruct((BLK, BLK), jnp.float32)
    return pl.pallas_call(
        pivots_kernel,
        out_shape=(shape, shape, shape),
        in_specs=[VMEM] * 2,
        out_specs=[VMEM] * 3,
        compiler_params=pltpu.CompilerParams(vmem_limit_bytes=32 << 20),
        cost_estimate=pl.CostEstimate(flops=25_000_000_000, bytes_accessed=1 << 20, transcendentals=0),
        name="factor_pivots",
    )(even, odd)


def columns_kernel(ids, pattern, y0, y1, inv00, u01, inv11, back0, back1, link, cols):
    for out, value in ((back0, inv00[...].T), (back1, inv11[...].T), (link, u01[...])):
        for number, part in enumerate(split(value, 2)):
            out[number] = part
    q = ids[1]
    swap = ids[2] == 1
    inverse0, inverse1, down = (split(inv00[...], 2), split(inv11[...], 2), split(u01[...].T, 2))
    for c in range(2):
        w = pattern[32 * c + q, 1].astype(jnp.float32)
        first = product(inverse0, split(jnp.where(swap, y1[c], y0[c]), 2), 2)
        left = jnp.where(swap, y0[c], y1[c]) - w * product(down, split(first, 2), 2)
        second = product(inverse1, split(left, 2), 2)
        for k, value in enumerate((first, second)):
            for number, part in enumerate(split(value, 2)):
                cols[c, number, k * BLK : (k + 1) * BLK, :] = part


def solve_columns(ids, pattern, y0, y1, inv00, u01, inv11):
    smem = pl.BlockSpec(memory_space=pltpu.SMEM)
    parts = jax.ShapeDtypeStruct((2, BLK, BLK), jnp.bfloat16)
    return pl.pallas_call(
        columns_kernel,
        out_shape=(parts, parts, parts, jax.ShapeDtypeStruct((2, 2, 2 * BLK, BLK), jnp.bfloat16)),
        in_specs=[smem, smem] + [VMEM] * 5,
        out_specs=[VMEM] * 4,
        compiler_params=pltpu.CompilerParams(vmem_limit_bytes=32 << 20),
        cost_estimate=pl.CostEstimate(flops=3_000_000_000, bytes_accessed=4 << 20, transcendentals=0),
        name="solve_columns",
    )(ids, pattern, y0, y1, inv00, u01, inv11)


def update_kernel(ids, pattern, local, g, back0, back1, link, cols, out):
    j = pl.program_id(0)
    p, q = (ids[0], ids[1])
    slots = [(ids[3] + 4 - m) % 4 for m in range(4)]
    raw = [jnp.concatenate([g[k, slot] for slot in slots], axis=0) for k in range(2)]
    first = product(split(raw[0], 2), back0, 2)
    x0 = split(first, 2)
    linked = product(x0, link, 2)
    w = [pattern[(j + 4 * h) * 8 + p, 1].astype(jnp.float32) for h in range(2)]
    left = [raw[1][h * BLK : (h + 1) * BLK] - w[h] * linked[h * BLK : (h + 1) * BLK] for h in range(2)]
    second = product(split(jnp.concatenate(left, axis=0), 2), back1, 2)
    x1 = split(second, 2)
    solved = [jnp.concatenate([x0[k], x1[k]], axis=1) for k in range(2)]
    for h in range(2):
        row_id = (j + 4 * h) * 8 + p
        rows = slice(h * BLK, (h + 1) * BLK)
        for c in range(2):
            col_id = 32 * c + q
            places = [pl.ds(2 * c + side, BLK, stride=4) for side in range(2)]
            halves = [slice(side * HALF, (side + 1) * HALF) for side in range(2)]
            panel = col_id < 2
            lower = row_id >= col_id
            changed = lower & ~panel & (pattern[row_id, col_id] != 0)

            @pl.when(panel)
            def _():
                r = lax.broadcasted_iota(jnp.int32, (BLK, BLK), 0)
                s = lax.broadcasted_iota(jnp.int32, (BLK, BLK), 1)
                kept = (row_id > col_id) | ((row_id == col_id) & (s <= r))
                value = jnp.where(kept, jnp.where(col_id == 0, first[rows], second[rows]), 0.0)
                for side in range(2):
                    out[h, 0, places[side], :] = value[:, halves[side]]

            @pl.when(~panel & ~lower)
            def _():
                for side in range(2):
                    out[h, 0, places[side], :] = jnp.zeros((BLK, HALF), jnp.float32)

            @pl.when(changed)
            def _():
                change = product([part[rows] for part in solved], cols[c], 2)
                for side in range(2):
                    out[h, 0, places[side], :] = local[h, 0, places[side], :] - change[:, halves[side]]

            @pl.when(lower & ~panel & ~changed)
            def _():
                for side in range(2):
                    out[h, 0, places[side], :] = local[h, 0, places[side], :]


def update(ids, pattern, local, g, back0, back1, link, cols):
    block = pl.BlockSpec((2, 1, 4 * BLK, HALF), lambda j, *_: (0, j, 0, 0))
    return pl.pallas_call(
        update_kernel,
        out_shape=jax.ShapeDtypeStruct(local.shape, jnp.float32),
        grid_spec=pltpu.PrefetchScalarGridSpec(
            num_scalar_prefetch=2,
            grid=(4,),
            in_specs=[
                block,
                pl.BlockSpec((2, 4, HALF, BLK), lambda j, *_: (j, 0, 0, 0)),
                *[VMEM] * 4,
            ],
            out_specs=block,
        ),
        compiler_params=pltpu.CompilerParams(vmem_limit_bytes=50 << 20),
        cost_estimate=pl.CostEstimate(flops=12_000_000_000, bytes_accessed=14 << 20, transcendentals=0),
        name="update",
    )(ids, pattern, local, g, back0, back1, link, cols)


def shifted(value, x=0, core=0, z=0, y=0, where=None):
    pairs = []
    for place in np.ndindex(NX, NCORE, NZ, NY):
        if where is None or where(*place):
            a, b, c, d = place
            to = ((a + x) % NX, (b + core) % NCORE, (c + z) % NZ, (d + y) % NY)
            pairs.append((int(DEVICE[place]), int(DEVICE[to])))
    return lax.ppermute(value, AXES, pairs)


def pick(index, choices):
    value = choices[0]
    for number, choice in enumerate(choices[1:], 1):
        value = jnp.where(index == number, choice, value)
    return value


def per_device(matrix, pattern):
    tie = lambda *arrays: lax.optimization_barrier(arrays)
    p = lax.axis_index("row")
    q = lax.axis_index("col")
    x, core, z, y = (p // NCORE, p % NCORE, q // NY, q % NY)
    local = matrix.reshape(2, 4, 4 * BLK, HALF)
    head = matrix[0, 0, :, :, 0, :].transpose(1, 0, 2)
    quarters = head.transpose(0, 2, 1).reshape(4, HALF, BLK)

    corner = head[0]
    own = jnp.stack([corner[:HALF, :HALF], corner[:HALF, HALF:], corner[HALF:, HALF:]])
    along = [shifted(own, x=k, where=lambda a, b, c, d: a == 0 and c == 0 and d < 2) for k in (1, 3, 2)]
    parts = []
    for m in range(4):
        pairs = [(32 * c + s, (s % 8) * 32 + 8 * (s // 8) + 4 * c + m) for c in range(2) for s in range(32)]
        parts.append(lax.ppermute(quarters[m], AXES, pairs))
    pivot = jnp.where((x == 0) & (z == 0) & (y < 2), own, 0.0) + along[0] + along[1] + along[2]
    along = [shifted(pivot, z=k, where=lambda a, b, c, d: c == 0 and d < 2) for k in (2, 6, 4)]
    pivot = pivot + along[0] + along[1] + along[2]
    mine = parts[0] + parts[1] + parts[2] + parts[3]
    mine, pivot = tie(mine, pivot)

    pivot = pivot + shifted(pivot, z=1, where=lambda a, b, c, d: c % 2 == 0 and d < 2)
    turns = [shifted(mine, y=k) for k in (1, 2, 3)]
    g = jnp.stack([mine] + turns)

    groups = [[NY * b + a for b in range(NZ)] for a in range(NY)]
    g = lax.all_gather(g, "col", axis=0, axis_index_groups=groups)
    got = [pivot] + [shifted(pivot, y=k, where=lambda a, b, c, d: d < 2) for k in (1, 2, 3)]
    both = jnp.stack([pick(y, got), pick((y + 3) % 4, got)])
    swapped = shifted(both, core=1)
    even = jnp.where(core == 0, both, swapped)
    odd = jnp.where(core == 0, swapped, both)
    even, odd, head = tie(even, odd, head)

    cols = [head] + [shifted(head, x=k, where=lambda a, *_: a == 0) for k in (1, 2, 3)]
    inv00, u01, inv11 = factor_pivots(even, odd)
    inv00, u01, inv11, cols[0] = tie(inv00, u01, inv11, cols[0])
    cols = pick(x, cols)
    other = shifted(cols, core=1)
    ids = jnp.stack([p, q, core, y]).astype(jnp.int32)
    solved = solve_columns(ids, pattern, cols, other, inv00, u01, inv11)
    solved, g = tie(solved, g)
    out = update(ids, pattern, local, g, *solved)
    return out.reshape(matrix.shape)


def solution(mesh):
    return jax.shard_map(
        per_device,
        mesh=mesh,
        in_specs=(P(None, "row", None, None, "col", None), P()),
        out_specs=P(None, "row", None, None, "col", None),
        check_vma=False,
    )
```

```python
import functools

import jax
import jax.numpy as jnp
import numpy as np
from jax import lax
from jax.experimental import pallas as pl
from jax.experimental.pallas import tpu as pltpu
from jax.sharding import PartitionSpec as P

AXES = ("row", "col")
NX, NCORE, NZ, NY = (4, 2, 8, 4)
BLK = 256
HALF = 128
STEP = 8
DEVICE = np.arange(NX * NCORE * NZ * NY).reshape(NX, NCORE, NZ, NY)
VMEM = pl.BlockSpec(memory_space=pltpu.VMEM)


LEFT = {3: (0, 0, 1, 0, 1, 2), 2: (0, 1, 0)}
RIGHT = {3: (0, 1, 0, 2, 1, 0), 2: (0, 0, 1)}


def split(value, count=3):
    parts = []
    for number in range(count):
        parts.append(value.astype(jnp.bfloat16))
        if number + 1 < count:
            value = value - parts[-1].astype(jnp.float32)
    return parts


def product(left, right, count=3):
    a = jnp.concatenate([left[k] for k in LEFT[count]], axis=1)
    b = jnp.concatenate([right[k] for k in RIGHT[count]], axis=0)
    return jnp.dot(a, b, preferred_element_type=jnp.float32)


def dot(a, b):
    return product(split(a), split(b))


def invert_factor(block):
    n = block.shape[0]
    lane = lax.broadcasted_iota(jnp.int32, (8, n), 1)
    sub = lax.broadcasted_iota(jnp.int32, (8, n), 0)
    rows = [block[8 * g : 8 * g + 8, :] for g in range(n // 8)]
    for first in range(0, n, STEP):
        top, at = divmod(first, 8)
        inside = (lane >= first) & (lane < first + STEP)
        low = range(top, n // 8)
        column = {
            g: [jnp.broadcast_to(rows[g][:, first + k : first + k + 1], (8, n)) for k in range(STEP)] for g in low
        }
        pivot = [
            [jnp.broadcast_to(column[top][k][at + i : at + i + 1, :], (8, n)) for k in range(i + 1)]
            for i in range(STEP)
        ]
        upper = [
            jnp.where(
                inside,
                (lane == first + k).astype(jnp.float32),
                jnp.broadcast_to(rows[top][at + k : at + k + 1, :], (8, n)),
            )
            for k in range(STEP)
        ]
        inverse = []
        for k in range(STEP):
            inverse.append(1.0 / pivot[k][k])
            for i in range(k + 1, STEP):
                ratio = pivot[i][k] * inverse[k]
                for m in range(k + 1, i + 1):
                    pivot[i][m] = pivot[i][m] - ratio * pivot[m][k]
                upper[i] = upper[i] - ratio * upper[k]
                for g in low:
                    column[g][i] = column[g][i] - ratio * column[g][k]
        scaled = [upper[k] * inverse[k] for k in range(STEP)]
        for g in low:
            left = jnp.where(inside, 0.0, rows[g])
            for k in range(STEP):
                left = left - column[g][k] * scaled[k]
            if g == top:
                done = rows[g]
                for k in range(STEP):
                    done = jnp.where(sub == at + k, upper[k] * lax.rsqrt(pivot[k][k]), done)
                left = jnp.where(sub >= at + STEP, left, done)
            rows[g] = left
    whole = jnp.concatenate(rows, axis=0)
    r = lax.broadcasted_iota(jnp.int32, (n, n), 0)
    c = lax.broadcasted_iota(jnp.int32, (n, n), 1)
    return jnp.where(c <= r, whole, 0.0)


def invert_pair(blocks, out):
    h = HALF
    top = invert_factor(blocks[0])
    link = dot(top, blocks[1])
    low = invert_factor(blocks[2] - dot(link.T, link))
    out[:h, :h] = top
    out[:h, h:] = jnp.zeros((h, h), jnp.float32)
    out[h:, :h] = -dot(dot(low, link.T), top)
    out[h:, h:] = low


def pivots_kernel(even, odd, inv00, u01, inv11):
    h = HALF
    invert_pair([even[0, k] for k in range(3)], inv00)
    upper = jnp.concatenate([even[1, 0], even[1, 1]], axis=1)
    lower = jnp.concatenate([odd[0, 1].T, odd[0, 2].T], axis=1)
    link = dot(inv00[...], jnp.concatenate([upper, lower], axis=0))
    u01[...] = link
    change = dot(link.T, link)
    parts = (change[:h, :h], change[:h, h:], change[h:, h:])
    invert_pair([odd[1, k] - parts[k] for k in range(3)], inv11)


def factor_pivots(even, odd):
    shape = jax.ShapeDtypeStruct((BLK, BLK), jnp.float32)
    return pl.pallas_call(
        pivots_kernel,
        out_shape=(shape, shape, shape),
        in_specs=[VMEM] * 2,
        out_specs=[VMEM] * 3,
        compiler_params=pltpu.CompilerParams(vmem_limit_bytes=32 << 20),
        cost_estimate=pl.CostEstimate(flops=25_000_000_000, bytes_accessed=1 << 20, transcendentals=0),
        name="factor_pivots",
    )(even, odd)


def columns_kernel(ids, pattern, y0, y1, inv00, u01, inv11, back0, back1, link, cols):
    for out, value in ((back0, inv00[...].T), (back1, inv11[...].T), (link, u01[...])):
        for number, part in enumerate(split(value, 2)):
            out[number] = part
    q = ids[1]
    swap = ids[2] == 1
    inverse0, inverse1, down = (split(inv00[...], 2), split(inv11[...], 2), split(u01[...].T, 2))
    for c in range(2):
        w = pattern[32 * c + q, 1].astype(jnp.float32)
        first = product(inverse0, split(jnp.where(swap, y1[c], y0[c]), 2), 2)
        left = jnp.where(swap, y0[c], y1[c]) - w * product(down, split(first, 2), 2)
        second = product(inverse1, split(left, 2), 2)
        for k, value in enumerate((first, second)):
            for number, part in enumerate(split(value, 2)):
                cols[c, number, k * BLK : (k + 1) * BLK, :] = part


def solve_columns(ids, pattern, y0, y1, inv00, u01, inv11):
    smem = pl.BlockSpec(memory_space=pltpu.SMEM)
    parts = jax.ShapeDtypeStruct((2, BLK, BLK), jnp.bfloat16)
    return pl.pallas_call(
        columns_kernel,
        out_shape=(parts, parts, parts, jax.ShapeDtypeStruct((2, 2, 2 * BLK, BLK), jnp.bfloat16)),
        in_specs=[smem, smem] + [VMEM] * 5,
        out_specs=[VMEM] * 4,
        compiler_params=pltpu.CompilerParams(vmem_limit_bytes=32 << 20),
        cost_estimate=pl.CostEstimate(flops=3_000_000_000, bytes_accessed=4 << 20, transcendentals=0),
        name="solve_columns",
    )(ids, pattern, y0, y1, inv00, u01, inv11)


def update_kernel(ids, pattern, local, g, back0, back1, link, cols, out):
    j = pl.program_id(0)
    p, q = (ids[0], ids[1])
    slots = [(ids[3] + 4 - m) % 4 for m in range(4)]
    raw = [jnp.concatenate([g[k, slot] for slot in slots], axis=0) for k in range(2)]
    first = product(split(raw[0], 2), back0, 2)
    x0 = split(first, 2)
    linked = product(x0, link, 2)
    w = [pattern[(j + 4 * h) * 8 + p, 1].astype(jnp.float32) for h in range(2)]
    left = [raw[1][h * BLK : (h + 1) * BLK] - w[h] * linked[h * BLK : (h + 1) * BLK] for h in range(2)]
    second = product(split(jnp.concatenate(left, axis=0), 2), back1, 2)
    x1 = split(second, 2)
    solved = [jnp.concatenate([x0[k], x1[k]], axis=1) for k in range(2)]
    for h in range(2):
        row_id = (j + 4 * h) * 8 + p
        rows = slice(h * BLK, (h + 1) * BLK)
        for c in range(2):
            col_id = 32 * c + q
            places = [pl.ds(2 * c + side, BLK, stride=4) for side in range(2)]
            halves = [slice(side * HALF, (side + 1) * HALF) for side in range(2)]
            panel = col_id < 2
            lower = row_id >= col_id
            changed = lower & ~panel & (pattern[row_id, col_id] != 0)

            @pl.when(panel)
            def _():
                r = lax.broadcasted_iota(jnp.int32, (BLK, BLK), 0)
                s = lax.broadcasted_iota(jnp.int32, (BLK, BLK), 1)
                kept = (row_id > col_id) | ((row_id == col_id) & (s <= r))
                value = jnp.where(kept, jnp.where(col_id == 0, first[rows], second[rows]), 0.0)
                for side in range(2):
                    out[h, 0, places[side], :] = value[:, halves[side]]

            @pl.when(~panel & ~lower)
            def _():
                for side in range(2):
                    out[h, 0, places[side], :] = jnp.zeros((BLK, HALF), jnp.float32)

            @pl.when(changed)
            def _():
                change = product([part[rows] for part in solved], cols[c], 2)
                for side in range(2):
                    out[h, 0, places[side], :] = local[h, 0, places[side], :] - change[:, halves[side]]

            @pl.when(lower & ~panel & ~changed)
            def _():
                for side in range(2):
                    out[h, 0, places[side], :] = local[h, 0, places[side], :]


def update(ids, pattern, local, g, back0, back1, link, cols):
    block = pl.BlockSpec((2, 1, 4 * BLK, HALF), lambda j, *_: (0, j, 0, 0))
    return pl.pallas_call(
        update_kernel,
        out_shape=jax.ShapeDtypeStruct(local.shape, jnp.float32),
        grid_spec=pltpu.PrefetchScalarGridSpec(
            num_scalar_prefetch=2,
            grid=(4,),
            in_specs=[
                block,
                pl.BlockSpec((2, 4, HALF, BLK), lambda j, *_: (j, 0, 0, 0)),
                *[VMEM] * 4,
            ],
            out_specs=block,
        ),
        compiler_params=pltpu.CompilerParams(vmem_limit_bytes=50 << 20),
        cost_estimate=pl.CostEstimate(flops=12_000_000_000, bytes_accessed=14 << 20, transcendentals=0),
        name="update",
    )(ids, pattern, local, g, back0, back1, link, cols)


def shifted(value, x=0, core=0, z=0, y=0, where=None):
    pairs = []
    for place in np.ndindex(NX, NCORE, NZ, NY):
        if where is None or where(*place):
            a, b, c, d = place
            to = ((a + x) % NX, (b + core) % NCORE, (c + z) % NZ, (d + y) % NY)
            pairs.append((int(DEVICE[place]), int(DEVICE[to])))
    return lax.ppermute(value, AXES, pairs)


def pick(index, choices):
    value = choices[0]
    for number, choice in enumerate(choices[1:], 1):
        value = jnp.where(index == number, choice, value)
    return value


def per_device(matrix, pattern):
    tie = lambda *arrays: lax.optimization_barrier(arrays)
    p = lax.axis_index("row")
    q = lax.axis_index("col")
    x, core, z, y = (p // NCORE, p % NCORE, q // NY, q % NY)
    local = matrix.reshape(2, 4, 4 * BLK, HALF)
    head = matrix[0, 0, :, :, 0, :].transpose(1, 0, 2)
    quarters = head.transpose(0, 2, 1).reshape(4, HALF, BLK)

    corner = head[0]
    own = jnp.stack([corner[:HALF, :HALF], corner[:HALF, HALF:], corner[HALF:, HALF:]])
    along = [shifted(own, x=k, where=lambda a, b, c, d: a == 0 and c == 0 and d < 2) for k in (1, 2, 3)]
    parts = []
    for m in range(4):
        pairs = [(32 * c + s, (s % 8) * 32 + 8 * (s // 8) + 4 * c + m) for c in range(2) for s in range(32)]
        parts.append(lax.ppermute(quarters[m], AXES, pairs))
    pivot = jnp.where((x == 0) & (z == 0) & (y < 2), own, 0.0) + along[0] + along[1] + along[2]
    along = [shifted(pivot, z=k, where=lambda a, b, c, d: c == 0 and d < 2) for k in (2, 6, 4)]
    pivot = pivot + along[0] + along[1] + along[2]
    mine = parts[0] + parts[1] + parts[2] + parts[3]
    mine, pivot = tie(mine, pivot)

    pivot = pivot + shifted(pivot, z=1, where=lambda a, b, c, d: c % 2 == 0 and d < 2)
    turns = {k: shifted(mine, y=k) for k in (1, 3, 2)}
    g = jnp.stack([mine] + [turns[k] for k in (1, 2, 3)])

    groups = [[NY * b + a for b in range(NZ)] for a in range(NY)]
    g = lax.all_gather(g, "col", axis=0, axis_index_groups=groups)
    turns = {k: shifted(pivot, y=k, where=lambda a, b, c, d: d < 2) for k in (1, 3, 2)}
    got = [pivot] + [turns[k] for k in (1, 2, 3)]
    both = jnp.stack([pick(y, got), pick((y + 3) % 4, got)])
    swapped = shifted(both, core=1)
    even = jnp.where(core == 0, both, swapped)
    odd = jnp.where(core == 0, swapped, both)
    even, odd, head = tie(even, odd, head)

    cols = [head] + [shifted(head, x=k, where=lambda a, *_: a == 0) for k in (1, 2, 3)]
    inv00, u01, inv11 = factor_pivots(even, odd)
    inv00, u01, inv11, cols[0] = tie(inv00, u01, inv11, cols[0])
    cols = pick(x, cols)
    other = shifted(cols, core=1)
    ids = jnp.stack([p, q, core, y]).astype(jnp.int32)
    solved = solve_columns(ids, pattern, cols, other, inv00, u01, inv11)
    solved, g = tie(solved, g)
    out = update(ids, pattern, local, g, *solved)
    return out.reshape(matrix.shape)


def solution(mesh):
    return jax.shard_map(
        per_device,
        mesh=mesh,
        in_specs=(P(None, "row", None, None, "col", None), P()),
        out_specs=P(None, "row", None, None, "col", None),
        check_vma=False,
    )
```
